128 devices in a mesh: dp: 16 (over y, x), seq: 8 (over z, core).
Axes of the slice: x: 4, y: 4, z: 4, core: 2. Of those that a mesh axis runs over, the one named last changes fastest.
Arguments:
- query_tokens: bfloat16 [2048, 512], P('dp'), may hold values from -16 to 16
- owner: int32 [2048], P('dp'), may hold values from 0 to 1
- d_out: bfloat16 [2048, 512], P('dp'), may hold values from -6 to 6
- history: bfloat16 [32, 16384, 512], P('dp', 'seq'), may hold values from -16 to 16
- lengths: int32 [32], P('dp'), may hold values from 2048 to 16384, as said below
- w_query: bfloat16 [512, 512], replicated, may hold values from -1 to 1
- w_key: bfloat16 [512, 512], replicated, may hold values from -1 to 1
- w_value: bfloat16 [512, 512], replicated, may hold values from -0.25 to 0.25
- w_out: bfloat16 [512, 512], replicated, may hold values from -0.25 to 0.25
Outputs:
- query_grad: bfloat16 [2048, 512], P('dp')
- hist_grad: bfloat16 [32, 16384, 512], P('dp', 'seq')
- weight_grads: float32 [512, 4, 512], P(('dp', 'seq'))
The draws below stay inside these ranges and needn't reach their ends.
Inputs may be any that keep to these rules, and one draw needn't show every extreme that they name: lengths are at least 2048; some request is full.
All inputs are finite; a program needn't handle non-finite values.
Results may differ from the reference program's by a relative error of at most 0.007.
The reference program's roundings to bfloat16 on the way count: a program that leaves them out, or rounds other values in their place, can miss the bound.
Values sent between devices are 32-bit elements; how exact they have to be, the bound alone decides.
No kernel may reach another device: no remote copies, remote signals or barrier semaphores. Data moves between devices by JAX's collectives and lax.ppermute only.
A program may use at most 128 MiB of HBM per device.

```python
import math
import jax
import jax.numpy as jnp
from jax import lax

D = 512
HEADS = 8
HD = 64
REQ_DEV = 2
HIST = 16384
REQS = 32
ROWS = 2048
N_DP = 16


def shared_weight(key):
    base = jnp.clip(jax.random.normal(jax.random.fold_in(key, 200), (D, D), jnp.float32), -6.0, 6.0)
    return base * (1.0 / math.sqrt(D))


def draw_query_tokens(key, part):
    key = jax.random.fold_in(key, 1)
    values = jnp.clip(jax.random.normal(key, (ROWS, D), jnp.float32), -6.0, 6.0)
    return values.astype(jnp.bfloat16)


def draw_history(key, part):
    key = jax.random.fold_in(key, 3)
    values = jnp.clip(jax.random.normal(key, (REQS, HIST, D), jnp.float32), -6.0, 6.0)
    return values.astype(jnp.bfloat16)


def draw_w_key(key, part):
    weight = shared_weight(key)
    return weight.astype(jnp.bfloat16)


def draw_w_query(key, part):
    key = jax.random.fold_in(key, 5)
    own = jnp.clip(jax.random.normal(key, (D, D), jnp.float32), -6.0, 6.0) * (1.0 / math.sqrt(D))
    return own.astype(jnp.bfloat16)


def draw_lengths(key, part):
    key = jax.random.fold_in(key, 6)
    drawn = jax.random.randint(key, (REQS,), HIST // 8, HIST + 1)
    top = jax.random.randint(jax.random.fold_in(key, 7), (), 0, REQS)
    low = (top + 1 + jax.random.randint(jax.random.fold_in(key, 8), (), 0, REQS - 1)) % REQS
    index = jnp.arange(REQS)
    drawn = jnp.where(index == top, HIST, jnp.where(index == low, HIST // 8, drawn))
    return drawn.astype(jnp.int32)


def with_ends(array, own_key, low, largest):
    shape = array.shape
    spot = [jax.random.randint(jax.random.fold_in(own_key, axis), (), 0, shape[axis]) for axis in range(len(shape))]
    array = array.at[tuple(spot)].set(low)
    longest = shape.index(max(shape))
    spot[longest] = (spot[longest] + 1) % shape[longest]
    return array.at[tuple(spot)].set(largest)


def block_levels(own_key, shape, shards, low, high):
    def one(dim, parts):
        steps = jax.random.uniform(jax.random.fold_in(jax.random.fold_in(own_key, 6), dim), (parts,), jnp.float32, low / len(shards), high / len(shards))
        return jnp.repeat(jnp.exp(steps), shape[dim] // parts).reshape((-1,) + (1,) * (len(shape) - dim - 1))

    gain = one(*shards[0])
    for cut in shards[1:]:
        gain = gain * one(*cut)
    return gain


def normal_values(rng, extent, scale, bound, shards=(), held_as=jnp.bfloat16):
    values = jax.random.normal(rng, extent, jnp.float32) * scale
    if len(shards) > 0:
        values = block_levels(rng, extent, shards, -0.22, 0.18) * values
    return jnp.clip(values, min=-bound, max=bound).astype(held_as)


def setup_inputs(seed: int = 0) -> dict:
    keys = jax.random.split(jax.random.key(seed), 10)
    return {
        "query_tokens": draw_query_tokens(jax.random.fold_in(keys[9], 71), 0),
        "owner": with_ends(jax.random.randint(keys[1], (ROWS,), 0, REQ_DEV), jax.random.fold_in(keys[1], 1), 0, REQ_DEV - 1).astype(jnp.int32),
        "d_out": normal_values(keys[2], (ROWS, D), 1.0, 6.0, ((0, 16),)),
        "history": draw_history(jax.random.fold_in(keys[9], 71), 0),
        "lengths": draw_lengths(jax.random.fold_in(keys[9], 71), 0),
        "w_query": draw_w_query(jax.random.fold_in(keys[9], 71), 0),
        "w_key": draw_w_key(jax.random.fold_in(keys[9], 71), 0),
        "w_value": normal_values(keys[7], (D, D), D ** -0.5, 0.25),
        "w_out": normal_values(keys[8], (D, D), D ** -0.5, 0.25),
    }


def block_backward(tokens, own, cotangent, hist, lens, w_query, w_key, w_value, w_out):
    rows = tokens.shape[0]
    requests = hist.shape[0]
    events = hist.shape[1]
    flat = hist.reshape(requests * events, D)
    scale = HD ** -0.5
    q = jnp.dot(tokens, w_query, preferred_element_type=jnp.float32).astype(jnp.bfloat16)
    k = jnp.dot(flat, w_key, preferred_element_type=jnp.float32).astype(jnp.bfloat16)
    v = jnp.dot(flat, w_value, preferred_element_type=jnp.float32).astype(jnp.bfloat16)
    qh = q.astype(jnp.float32).reshape(rows, HEADS, HD)
    kh = k.astype(jnp.float32).reshape(-1, HEADS, HD)
    vh = v.astype(jnp.float32).reshape(-1, HEADS, HD)
    slot = jnp.arange(requests * events, dtype=jnp.int32)
    request = slot // events
    position = slot % events
    visible = (own[:, None] == request[None, :]) & (position < lens[request])[None, :]
    scores = jnp.einsum('qhd,khd->hqk', qh, kh) * scale
    peak = jnp.max(jnp.where(visible[None], scores, -jnp.inf), axis=2, keepdims=True)
    expo = jnp.where(visible[None], jnp.exp(scores - peak), 0.0)
    probs = expo / jnp.sum(expo, axis=2, keepdims=True)
    probs_low = probs.astype(jnp.bfloat16)
    attention = jnp.einsum('hqk,khd->qhd', probs_low.astype(jnp.float32), vh).reshape(rows, D)
    grad_attn = jnp.dot(cotangent, w_out.T, preferred_element_type=jnp.float32).astype(jnp.bfloat16)
    grad_heads = grad_attn.astype(jnp.float32).reshape(rows, HEADS, HD)
    delta = jnp.sum(grad_heads * attention.reshape(rows, HEADS, HD), axis=2).T
    slopes = jnp.einsum('qhd,khd->hqk', grad_heads, vh)
    dscore = (probs_low.astype(jnp.float32) * (slopes - delta[:, :, None])).astype(jnp.bfloat16)
    dq = (jnp.einsum('hqk,khd->qhd', dscore.astype(jnp.float32), kh) * scale).reshape(rows, D).astype(jnp.bfloat16)
    dk = (jnp.einsum('hqk,qhd->khd', dscore.astype(jnp.float32), qh) * scale).reshape(-1, D).astype(jnp.bfloat16)
    dv = jnp.einsum('hqk,qhd->khd', probs_low.astype(jnp.float32), grad_heads).reshape(-1, D).astype(jnp.bfloat16)
    query_grad = jnp.dot(dq, w_query.T, preferred_element_type=jnp.float32).astype(jnp.bfloat16)
    hist_grad = (jnp.dot(dk, w_key.T, preferred_element_type=jnp.float32)
                 + jnp.dot(dv, w_value.T, preferred_element_type=jnp.float32)).astype(jnp.bfloat16)
    terms = jnp.stack([
        jnp.dot(tokens.T, dq, preferred_element_type=jnp.float32),
        jnp.dot(flat.T, dk, preferred_element_type=jnp.float32),
        jnp.dot(flat.T, dv, preferred_element_type=jnp.float32),
        jnp.dot(attention.astype(jnp.bfloat16).T, cotangent, preferred_element_type=jnp.float32),
    ], axis=1)
    return query_grad, hist_grad.reshape(requests, events, D), terms


def reference(query_tokens, owner, d_out, history, lengths, w_query, w_key, w_value, w_out):
    per = query_tokens.shape[0] // N_DP
    items = (query_tokens.reshape(N_DP, per, D), owner.reshape(N_DP, per), d_out.reshape(N_DP, per, D),
             history.reshape(N_DP, REQ_DEV, HIST, D), lengths.reshape(N_DP, REQ_DEV))

    def step(acc, item):
        query_grad, hist_grad, terms = block_backward(item[0], item[1], item[2], item[3], item[4],
                                                      w_query, w_key, w_value, w_out)
        return acc + terms, (query_grad, hist_grad)

    total, outs = lax.scan(step, jnp.zeros((D, 4, D), jnp.float32), items)
    return outs[0].reshape(ROWS, D), outs[1].reshape(REQS, HIST, D), total
```

```python
import jax
import jax.numpy as jnp
from jax import lax
from jax.experimental import pallas as pl
from jax.experimental.pallas import tpu as pltpu
from jax.sharding import PartitionSpec as P

HEADS = 8
PAIRS = 4
LOW = -1e30
F32 = jnp.float32
BF16 = jnp.bfloat16
TILE = 512


def dot(left, right):
    return jnp.dot(left, right, preferred_element_type=F32)


def dot_last(left, right):
    return lax.dot_general(left, right, (((1,), (1,)), ((), ())), preferred_element_type=F32)


def dot_first(left, right):
    return lax.dot_general(left, right, (((0,), (0,)), ((), ())), preferred_element_type=F32)


def pair_cols(ref, pair):
    cols = slice(128 * pair, 128 * pair + 128)
    return jnp.concatenate([ref[0, :, cols], ref[1, :, cols]], axis=1)


def spread(rows, own_col, owner_row, blk_ref, blk_t_ref):
    lane = lax.broadcasted_iota(jnp.int32, (128, 128), 1)
    zero = jnp.zeros((64, 128), F32)
    for pair in range(PAIRS):
        part = rows[:, 128 * pair : 128 * pair + 128]
        part_t = part.T
        for req in range(2):
            mine = jnp.where(own_col == req, part, 0.0)
            cols = slice(128 * req, 128 * req + 128)
            blk_t_ref[pair, 0:128, cols] = jnp.where(lane < 64, mine, 0.0).astype(BF16)
            blk_t_ref[pair, 128:256, cols] = jnp.where(lane < 64, 0.0, mine).astype(BF16)
            mine_t = jnp.where(owner_row == req, part_t, 0.0)
            top = jnp.concatenate([mine_t[0:64], zero], axis=1)
            low = jnp.concatenate([zero, mine_t[64:128]], axis=1)
            blk_ref[pair, cols, :] = jnp.concatenate([top, low], axis=0).astype(BF16)


def keys_kernel(lens_ref, tok_ref, wq_ref, dout_ref, wout_ref, own_ref, hist_ref, wk_ref,
                key_ref, stat_ref, lim_ref, qb_ref, qbt_ref, gb_ref, gbt_ref, peak, total):
    step = pl.program_id(0)
    tile = hist_ref.shape[1]
    events = tile * pl.num_programs(0)

    @pl.when(step == 0)
    def _():
        owner_row = jnp.broadcast_to(own_ref[...], (128, 128))
        own_col = owner_row.T
        base = lax.axis_index("seq") * events
        lim = jnp.where(own_ref[...] == 0, lens_ref[0], lens_ref[1]) - base
        lim_ref[...] = jnp.broadcast_to(jnp.concatenate([lim, lim], axis=1), (8, 256))
        q = dot(tok_ref[...], wq_ref[...]).astype(BF16).astype(F32) * 0.125
        spread(q, own_col, owner_row[0:1], qb_ref, qbt_ref)
        g = dot_last(dout_ref[...], wout_ref[...]).astype(BF16).astype(F32)
        spread(g, own_col, owner_row[0:1], gb_ref, gbt_ref)
        peak[...] = jnp.full(peak.shape, LOW, F32)
        total[...] = jnp.zeros(total.shape, F32)

    for req in range(2):
        key_ref[req] = dot(hist_ref[req], wk_ref[...]).astype(BF16)
    place = lax.broadcasted_iota(jnp.int32, (tile, 256), 0) + step * tile
    seen = place < lim_ref[0:1]
    for pair in range(PAIRS):
        score = dot(pair_cols(key_ref, pair), qb_ref[pair])
        score = jnp.where(seen, score, LOW)
        old = peak[pair : pair + 1]
        new = jnp.maximum(old, jnp.max(score, axis=0, keepdims=True))
        fresh = jnp.sum(jnp.exp(score - new), axis=0, keepdims=True)
        total[pair : pair + 1] = total[pair : pair + 1] * jnp.exp(old - new) + fresh
        peak[pair : pair + 1] = new

    @pl.when(step == pl.num_programs(0) - 1)
    def _():
        stats = jnp.concatenate([peak[0:4], total[0:4]], axis=0)
        for dev in range(8):
            stat_ref[dev] = stats


def values_kernel(hist_ref, wv_ref, val_ref):
    for req in range(2):
        val_ref[req] = dot(hist_ref[req], wv_ref[...]).astype(BF16)


def probs_kernel(stat_ref, lim_ref, qb_ref, gb_ref, key_ref, val_ref, prob_ref, delta_ref,
                 shift, delta):
    step = pl.program_id(0)
    tile = key_ref.shape[1]

    @pl.when(step == 0)
    def _():
        top = jnp.max(stat_ref[:, 0:4], axis=0)
        norm = jnp.sum(stat_ref[:, 4:8] * jnp.exp(stat_ref[:, 0:4] - top[None]), axis=0)
        shift[0:4] = top + jnp.log(norm)
        delta[...] = jnp.zeros(delta.shape, F32)

    place = lax.broadcasted_iota(jnp.int32, (tile, 256), 0) + step * tile
    seen = place < lim_ref[0:1]
    for pair in range(PAIRS):
        score = dot(pair_cols(key_ref, pair), qb_ref[pair])
        prob = jnp.where(seen, jnp.exp(score - shift[pair : pair + 1]), 0.0).astype(BF16)
        prob_ref[:, 256 * pair : 256 * pair + 256] = prob
        slope = dot(pair_cols(val_ref, pair), gb_ref[pair])
        delta[pair : pair + 1] += jnp.sum(prob.astype(F32) * slope, axis=0, keepdims=True)

    @pl.when(step == pl.num_programs(0) - 1)
    def _():
        for dev in range(8):
            delta_ref[dev] = delta[...]


def value_grads_kernel(own_ref, prob_ref, val_ref, hist_ref, gbt_ref, dv_ref, att_ref, wgrad_ref,
                       att):
    step = pl.program_id(0)

    @pl.when(step == 0)
    def _():
        att[...] = jnp.zeros(att.shape, F32)
        wgrad_ref[...] = jnp.zeros(wgrad_ref.shape, F32)

    for pair in range(PAIRS):
        prob = prob_ref[:, 256 * pair : 256 * pair + 256]
        grad = dot(prob, gbt_ref[pair]).astype(BF16)
        dv_ref[0, :, 128 * pair : 128 * pair + 128] = grad[:, 0:128]
        dv_ref[1, :, 128 * pair : 128 * pair + 128] = grad[:, 128:256]
        att[pair] += dot_first(pair_cols(val_ref, pair), prob)
    for req in range(2):
        wgrad_ref[...] += dot_first(hist_ref[req], dv_ref[req])

    @pl.when(step == pl.num_programs(0) - 1)
    def _():
        first = own_ref[...] == 0
        for pair in range(PAIRS):
            for head in range(2):
                lanes = slice(128 * head, 128 * head + 128)
                one = att[pair, 64 * head : 64 * head + 64, lanes]
                two = att[pair, 128 + 64 * head : 192 + 64 * head, lanes]
                out = jnp.where(first, one, two)
                for group in range(16):
                    feature = 128 * pair + 64 * head + 4 * group
                    dp, seq = feature // 32, (feature // 4) % 8
                    att_ref[seq, 4 * dp : 4 * dp + 4] = out[4 * group : 4 * group + 4]


def key_grads_kernel(own_ref, delta_ref, prob_ref, key_ref, val_ref, hist_ref, qbt_ref, gb_ref,
                     dk_ref, dq_ref, wgrad_ref, delta, dq):
    step = pl.program_id(0)

    @pl.when(step == 0)
    def _():
        delta[...] = jnp.sum(delta_ref[...], axis=0)
        dq[...] = jnp.zeros(dq.shape, F32)
        wgrad_ref[...] = jnp.zeros(wgrad_ref.shape, F32)

    for pair in range(PAIRS):
        prob = prob_ref[:, 256 * pair : 256 * pair + 256].astype(F32)
        slope = dot(pair_cols(val_ref, pair), gb_ref[pair])
        ds = (prob * (slope - delta[pair : pair + 1])).astype(BF16)
        dq[pair] += dot_first(ds, pair_cols(key_ref, pair))
        grad = dot(ds, qbt_ref[pair]).astype(BF16)
        dk_ref[0, :, 128 * pair : 128 * pair + 128] = grad[:, 0:128]
        dk_ref[1, :, 128 * pair : 128 * pair + 128] = grad[:, 128:256]
    for req in range(2):
        wgrad_ref[...] += dot_first(hist_ref[req], dk_ref[req])

    @pl.when(step == pl.num_programs(0) - 1)
    def _():
        own_col = jnp.broadcast_to(own_ref[...], (128, 128)).T
        lane = lax.broadcasted_iota(jnp.int32, (128, 128), 1)
        for pair in range(PAIRS):
            sel = jnp.where(own_col == 0, dq[pair, :128, :128], dq[pair, :128, 128:])
            sel2 = jnp.where(own_col == 0, dq[pair, 128:, :128], dq[pair, 128:, 128:])
            dq_ref[:, 128 * pair : 128 * pair + 128] = jnp.where(lane < 64, sel, sel2)


def hist_grads_kernel(dk_ref, dv_ref, wk_ref, wv_ref, out_ref):
    for req in range(2):
        out_ref[req] = (dot_last(dk_ref[req], wk_ref[...])
                        + dot_last(dv_ref[req], wv_ref[...])).astype(BF16)


def query_grads_kernel(dq_ref, wq_ref, tok_ref, att_ref, dout_ref, qgrad_ref, part_ref):
    dq = (dq_ref[...] * 0.125).astype(BF16)
    qgrad_ref[...] = dot_last(dq, wq_ref[...]).astype(BF16)
    row = lax.broadcasted_iota(jnp.int32, (64, 512), 0)
    col = lax.broadcasted_iota(jnp.int32, (64, 512), 1)
    feature = (row // 4) * 32 + lax.axis_index("seq") * 4 + row % 4
    pick = jnp.where(col == feature, 1.0, 0.0).astype(BF16)
    tok = dot_last(pick, tok_ref[...]).astype(BF16)
    first = dot(tok, dq)
    att = jnp.sum(att_ref[...], axis=0).astype(BF16)
    last = dot(att, dout_ref[...])
    for dp in range(16):
        part_ref[dp, 0:4] = first[4 * dp : 4 * dp + 4]
        part_ref[dp, 4:8] = last[4 * dp : 4 * dp + 4]


def whole(*shape):
    return pl.BlockSpec(shape, lambda i: (0,) * len(shape))


def tiles(tile, width):
    return pl.BlockSpec((2, tile, width), lambda i: (0, i, 0))


def call(kernel, steps, ins, outs, shapes, scratch=(), limit=48):
    return pl.pallas_call(
        kernel,
        grid=(steps,),
        in_specs=ins,
        out_specs=outs,
        out_shape=shapes,
        scratch_shapes=scratch,
        compiler_params=pltpu.CompilerParams(
            dimension_semantics=("arbitrary",), vmem_limit_bytes=limit * 1024 * 1024
        ),
    )


def sds(dtype, *shape):
    return jax.ShapeDtypeStruct(shape, dtype)


def per_device(query_tokens, owner, d_out, history, lengths, w_query, w_key, w_value, w_out):
    rows, width = query_tokens.shape
    requests, events, _ = history.shape
    tile = TILE
    steps = events // tile
    own = owner.reshape(1, rows)
    smem = pl.BlockSpec(memory_space=pltpu.SMEM)
    mat = whole(width, width)
    act = whole(rows, width)
    own_spec = whole(1, rows)
    ev = tiles(tile, width)
    blk = whole(PAIRS, 256, 256)
    prob_spec = pl.BlockSpec((tile, 1024), lambda i: (i, 0))
    ev_shape = sds(BF16, requests, events, width)
    blk_shape = sds(BF16, PAIRS, 256, 256)
    vec = whole(8, 8, 256)
    vec_shape = sds(F32, 8, 8, 256)

    keys, stats, lim, qb, qbt, gb, gbt = call(
        keys_kernel, steps,
        [smem, act, mat, act, mat, own_spec, ev, mat],
        [ev, vec, whole(8, 256), blk, blk, blk, blk],
        [ev_shape, vec_shape, sds(jnp.int32, 8, 256)] + [blk_shape] * 4,
        [pltpu.VMEM((8, 256), F32), pltpu.VMEM((8, 256), F32)],
    )(lengths, query_tokens, w_query, d_out, w_out, own, history, w_key)
    stats = lax.all_to_all(stats, "seq", 0, 0)
    values = call(values_kernel, steps, [ev, mat], ev, ev_shape)(history, w_value)

    probs, delta = call(
        probs_kernel, steps,
        [vec, whole(8, 256), blk, blk, ev, ev],
        [prob_spec, vec],
        [sds(BF16, events, 1024), vec_shape],
        [pltpu.VMEM((8, 256), F32), pltpu.VMEM((8, 256), F32)],
    )(stats, lim, qb, gb, keys, values)
    delta = lax.all_to_all(delta, "seq", 0, 0)

    dv, att, wgrad_v = call(
        value_grads_kernel, steps,
        [own_spec, prob_spec, ev, ev, blk],
        [ev, whole(8, 64, rows), mat],
        [ev_shape, sds(F32, 8, 64, rows), sds(F32, width, width)],
        [pltpu.VMEM((PAIRS, 256, 256), F32)],
    )(own, probs, values, history, gbt)
    att = lax.all_to_all(att, "seq", 0, 0)
    wgrad_v = lax.all_to_all(wgrad_v.reshape(16, 32, width), "dp", 0, 0)

    dk, dq, wgrad_k = call(
        key_grads_kernel, steps,
        [own_spec, vec, prob_spec, ev, ev, ev, blk, blk],
        [ev, act, mat],
        [ev_shape, sds(F32, rows, width), sds(F32, width, width)],
        [pltpu.VMEM((8, 256), F32), pltpu.VMEM((PAIRS, 256, 256), F32)],
    )(own, delta, probs, keys, values, history, qbt, gb)
    dq = lax.all_to_all(dq.reshape(8, 16, width), "seq", 0, 0)
    wgrad_k = lax.all_to_all(wgrad_k.reshape(16, 32, width), "dp", 0, 0)

    hist_grad = call(hist_grads_kernel, steps, [ev, ev, mat, mat], ev, ev_shape)(
        dk, dv, w_key, w_value)

    dq = jnp.sum(dq, axis=0)
    dq = lax.all_to_all(jnp.broadcast_to(dq[None], (8, 16, width)), "seq", 0, 0)
    dq = dq.reshape(rows, width)
    query_grad, outer = call(
        query_grads_kernel, 1,
        [act, mat, act, whole(8, 64, rows), act],
        [act, whole(16, 8, width)],
        [sds(BF16, rows, width), sds(F32, 16, 8, width)],
    )(dq, w_query, query_tokens, att, d_out)
    outer = jnp.sum(lax.all_to_all(outer, "dp", 0, 0), axis=0)

    inner = jnp.concatenate(
        [jnp.sum(wgrad_k, axis=0).reshape(8, 4, width), jnp.sum(wgrad_v, axis=0).reshape(8, 4, width)],
        axis=1)
    inner = jnp.sum(lax.all_to_all(inner, "seq", 0, 0), axis=0)
    weight_part = jnp.stack([outer[0:4], inner[0:4], inner[4:8], outer[4:8]], axis=1)
    return query_grad, hist_grad, weight_part


def solution(mesh):
    return jax.shard_map(
        per_device,
        mesh=mesh,
        in_specs=(
            P("dp", None),
            P("dp"),
            P("dp", None),
            P("dp", "seq", None),
            P("dp"),
            P(),
            P(),
            P(),
            P(),
        ),
        out_specs=(P("dp", None), P("dp", "seq", None), P(("dp", "seq"), None, None)),
        check_vma=False,
    )
```

```python
import jax
import jax.numpy as jnp
from jax import lax
from jax.experimental import pallas as pl
from jax.experimental.pallas import tpu as pltpu
from jax.sharding import PartitionSpec as P

PAIRS = 4
LOW = -1e30
F32 = jnp.float32
BF16 = jnp.bfloat16
VMEM = pltpu.MemorySpace.VMEM
HBM = pltpu.MemorySpace.HBM
TILE = 512


def dot(left, right):
    return jnp.dot(left, right, preferred_element_type=F32)


def dot_last(left, right):
    return lax.dot_general(left, right, (((1,), (1,)), ((), ())), preferred_element_type=F32)


def dot_first(left, right):
    return lax.dot_general(left, right, (((0,), (0,)), ((), ())), preferred_element_type=F32)


def tiles(ref):
    events = ref.shape[1]
    return [slice(start, start + TILE) for start in range(0, events, TILE)]


def pair_cols(ref, pair, rows):
    cols = slice(128 * pair, 128 * pair + 128)
    return jnp.concatenate([ref[0, rows, cols], ref[1, rows, cols]], axis=1)


def put_pair(ref, pair, rows, value):
    cols = slice(128 * pair, 128 * pair + 128)
    ref[0, rows, cols] = value[:, 0:128]
    ref[1, rows, cols] = value[:, 128:256]


def pair_lanes(pair):
    return slice(256 * pair, 256 * pair + 256)


def seen_in(lim_ref, rows):
    place = lax.broadcasted_iota(jnp.int32, (TILE, 256), 0) + rows.start
    return place < lim_ref[0:1]


def spread(full, own_col, owner_row, blk_ref, blk_t_ref):
    lane = lax.broadcasted_iota(jnp.int32, (128, 128), 1)
    zero = jnp.zeros((64, 128), F32)
    for pair in range(PAIRS):
        part = full[:, 128 * pair : 128 * pair + 128]
        part_t = part.T
        for req in range(2):
            mine = jnp.where(own_col == req, part, 0.0)
            cols = slice(128 * req, 128 * req + 128)
            blk_t_ref[pair, 0:128, cols] = jnp.where(lane < 64, mine, 0.0).astype(BF16)
            blk_t_ref[pair, 128:256, cols] = jnp.where(lane < 64, 0.0, mine).astype(BF16)
            mine_t = jnp.where(owner_row == req, part_t, 0.0)
            top = jnp.concatenate([mine_t[0:64], zero], axis=1)
            low = jnp.concatenate([zero, mine_t[64:128]], axis=1)
            blk_ref[pair, cols, :] = jnp.concatenate([top, low], axis=0).astype(BF16)


def keys_kernel(lens_ref, own_hbm, tok_hbm, wq_hbm, wk_hbm, hist_hbm,
                key_ref, hist_ref, stat_ref, lim_ref, qb_ref, own_ref, qbt_hbm,
                qbt_ref, tok_ref, wq_ref, wk_ref, sems):
    small = [(own_hbm, own_ref), (tok_hbm, tok_ref), (wq_hbm, wq_ref), (wk_hbm, wk_ref)]
    small = [pltpu.make_async_copy(src, dst, sems.at[i]) for i, (src, dst) in enumerate(small)]
    for copy in small:
        copy.start()
    chunks = []
    for rows in tiles(hist_ref):
        for req in range(2):
            copy = pltpu.make_async_copy(
                hist_hbm.at[req, rows], hist_ref.at[req, rows], sems.at[4 + len(chunks)])
            copy.start()
            chunks.append(copy)
    for copy in small:
        copy.wait()
    owner_row = jnp.broadcast_to(own_ref[...], (128, 128))
    base = lax.axis_index("seq") * hist_ref.shape[1]
    lim = jnp.where(own_ref[...] == 0, lens_ref[0], lens_ref[1]) - base
    lim_ref[...] = jnp.broadcast_to(jnp.concatenate([lim, lim], axis=1), (8, 256))
    q = dot(tok_ref[...], wq_ref[...]).astype(BF16).astype(F32) * 0.125
    spread(q, owner_row.T, owner_row[0:1], qb_ref, qbt_ref)
    qbt_copy = pltpu.make_async_copy(qbt_ref, qbt_hbm, sems.at[4 + len(chunks)])
    qbt_copy.start()

    peak = [jnp.full((1, 256), LOW, F32) for _ in range(PAIRS)]
    total = [jnp.zeros((1, 256), F32) for _ in range(PAIRS)]
    for index, rows in enumerate(tiles(hist_ref)):
        for req in range(2):
            chunks[2 * index + req].wait()
            key_ref[req, rows] = dot(hist_ref[req, rows], wk_ref[...]).astype(BF16)
        seen = seen_in(lim_ref, rows)
        for pair in range(PAIRS):
            score = jnp.where(seen, dot(pair_cols(key_ref, pair, rows), qb_ref[pair]), LOW)
            new = jnp.maximum(peak[pair], jnp.max(score, axis=0, keepdims=True))
            fresh = jnp.sum(jnp.exp(score - new), axis=0, keepdims=True)
            total[pair] = total[pair] * jnp.exp(peak[pair] - new) + fresh
            peak[pair] = new
    stat_ref[...] = jnp.concatenate(peak + total, axis=0)
    qbt_copy.wait()


def values_kernel(wv_hbm, dout_hbm, wout_hbm, own_ref, hist_ref,
                  val_ref, gb_ref, gbt_ref, wv_ref, dout_ref, wout_ref, sems):
    copies = [(wv_hbm, wv_ref), (dout_hbm, dout_ref), (wout_hbm, wout_ref)]
    copies = [pltpu.make_async_copy(src, dst, sems.at[i]) for i, (src, dst) in enumerate(copies)]
    for copy in copies:
        copy.start()
    copies[0].wait()
    for rows in tiles(hist_ref):
        for req in range(2):
            val_ref[req, rows] = dot(hist_ref[req, rows], wv_ref[...]).astype(BF16)
    copies[1].wait()
    copies[2].wait()
    owner_row = jnp.broadcast_to(own_ref[...], (128, 128))
    g = dot_last(dout_ref[...], wout_ref[...]).astype(BF16).astype(F32)
    spread(g, owner_row.T, owner_row[0:1], gb_ref, gbt_ref)


def probs_kernel(*refs):
    stats = refs[0:8]
    lim_ref, qb_ref, gb_ref, key_ref, val_ref, prob_ref, delta_ref = refs[8:]
    top = stats[0][0:4]
    for stat in stats[1:]:
        top = jnp.maximum(top, stat[0:4])
    norm = jnp.zeros((4, 256), F32)
    for stat in stats:
        norm += stat[4:8] * jnp.exp(stat[0:4] - top)
    shift = top + jnp.log(norm)
    delta = [jnp.zeros((1, 256), F32) for _ in range(PAIRS)]
    for rows in tiles(key_ref):
        seen = seen_in(lim_ref, rows)
        for pair in range(PAIRS):
            score = dot(pair_cols(key_ref, pair, rows), qb_ref[pair])
            prob = jnp.where(seen, jnp.exp(score - shift[pair : pair + 1]), 0.0).astype(BF16)
            prob_ref[rows, pair_lanes(pair)] = prob
            slope = dot(pair_cols(val_ref, pair, rows), gb_ref[pair])
            delta[pair] += jnp.sum(prob.astype(F32) * slope, axis=0, keepdims=True)
    delta_ref[...] = jnp.concatenate(delta + [jnp.zeros((4, 256), F32)], axis=0)


def put_shares(out_ref, value):
    for row in range(0, 512, 4):
        dp, seq = row // 32, (row // 4) % 8
        out_ref[seq, 4 * dp : 4 * dp + 4] = value[row : row + 4]


def put_shares(out_ref, value):
    for row in range(0, 512, 4):
        dp, seq = row // 32, (row // 4) % 8
        out_ref[seq, 4 * dp : 4 * dp + 4] = value[row : row + 4]


def halve(shares, keep_ref, send_ref):
    me = lax.axis_index("seq")
    for slot in range(4):
        chip = lax.rem(me // 2 + slot, 4)
        keep_ref[slot] = shares[2 * chip + lax.rem(me, 2)]
        send_ref[slot] = shares[2 * chip + 1 - lax.rem(me, 2)]


def value_grads_kernel(prob_ref, hist_ref, gbt_ref, dv_hbm, keep_ref, send_ref,
                       dv_ref, wgrad, shares, sems):
    copies = []
    for rows in tiles(hist_ref):
        for pair in range(PAIRS):
            grad = dot(prob_ref[rows, pair_lanes(pair)], gbt_ref[pair]).astype(BF16)
            put_pair(dv_ref, pair, rows, grad)
        for req in range(2):
            copy = pltpu.make_async_copy(
                dv_ref.at[req, rows], dv_hbm.at[req, rows], sems.at[len(copies)])
            copy.start()
            copies.append(copy)
    wgrad[...] = dot_first(hist_ref[0], dv_ref[0])
    wgrad[...] += dot_first(hist_ref[1], dv_ref[1])
    put_shares(shares, wgrad)
    halve(shares, keep_ref, send_ref)
    for copy in copies:
        copy.wait()


def attention_kernel(own_ref, prob_ref, val_ref, token_ref, att_ref):
    first = own_ref[...] == 0
    for pair in range(PAIRS):
        blk = jnp.zeros((256, 256), F32)
        for rows in tiles(val_ref):
            blk += dot_first(pair_cols(val_ref, pair, rows), prob_ref[rows, pair_lanes(pair)])
        for head in range(2):
            lanes = slice(128 * head, 128 * head + 128)
            one = blk[64 * head : 64 * head + 64, lanes]
            two = blk[128 + 64 * head : 192 + 64 * head, lanes]
            start = 128 * pair + 64 * head
            att_ref[start : start + 64] = jnp.where(first, one, two)


def query_part_kernel(*refs):
    deltas = refs[0:8]
    (own_ref, prob_ref, key_ref, val_ref, gb_ref, att_ref, keep_ref, recv_ref,
     ds_hbm, out_ref, part0, part1, part2, part3, ds_ref, sems) = refs[8:]
    delta = deltas[0][0:4]
    for other in deltas[1:]:
        delta += other[0:4]
    own_col = jnp.broadcast_to(own_ref[...], (128, 128)).T
    lane = lax.broadcasted_iota(jnp.int32, (128, 128), 1)
    copies = []
    blks = [jnp.zeros((256, 256), F32) for _ in range(PAIRS)]
    for rows in tiles(key_ref):
        for pair in range(PAIRS):
            prob = prob_ref[rows, pair_lanes(pair)].astype(F32)
            slope = dot(pair_cols(val_ref, pair, rows), gb_ref[pair])
            ds = (prob * (slope - delta[pair : pair + 1])).astype(BF16)
            ds_ref[rows, pair_lanes(pair)] = ds
            blks[pair] += dot_first(ds, pair_cols(key_ref, pair, rows))
        copy = pltpu.make_async_copy(ds_ref.at[rows], ds_hbm.at[rows], sems.at[len(copies)])
        copy.start()
        copies.append(copy)
    for pair in range(PAIRS):
        blk = blks[pair]
        one = jnp.where(own_col == 0, blk[:128, :128], blk[:128, 128:])
        two = jnp.where(own_col == 0, blk[128:, :128], blk[128:, 128:])
        dq = jnp.where(lane < 64, one, two)
        for dev in range(8):
            out_ref[dev, 0:16, 128 * pair : 128 * pair + 128] = dq[16 * dev : 16 * dev + 16]
    for row in range(0, 512, 4):
        dp, seq = row // 32, (row // 4) % 8
        lanes = slice(128 * (dp // 4), 128 * (dp // 4) + 128)
        start = 16 + 4 * (dp % 4)
        out_ref[seq, start : start + 4, lanes] = att_ref[row : row + 4]
    for slot, part in enumerate((part0, part1, part2, part3)):
        part[...] = keep_ref[slot] + recv_ref[slot]
    for copy in copies:
        copy.wait()


def key_grads_kernel(ds_hbm, hist_hbm, qbt_hbm, dk_hbm, keep_ref, send_ref,
                     ds_ref, hist_ref, qbt_ref, dk_ref, wgrad, shares, sems, out_sems):
    first = pltpu.make_async_copy(qbt_hbm, qbt_ref, sems.at[0])
    first.start()
    ins = []
    for index, rows in enumerate(tiles(hist_ref)):
        copy = pltpu.make_async_copy(ds_hbm.at[rows], ds_ref.at[rows], sems.at[1 + index])
        copy.start()
        ins.append(copy)
    loads = []
    for req in range(2):
        copy = pltpu.make_async_copy(
            hist_hbm.at[req], hist_ref.at[req], sems.at[1 + len(ins) + req])
        copy.start()
        loads.append(copy)
    first.wait()
    outs = []
    for index, rows in enumerate(tiles(hist_ref)):
        ins[index].wait()
        for pair in range(PAIRS):
            grad = dot(ds_ref[rows, pair_lanes(pair)], qbt_ref[pair]).astype(BF16)
            put_pair(dk_ref, pair, rows, grad)
        for req in range(2):
            copy = pltpu.make_async_copy(
                dk_ref.at[req, rows], dk_hbm.at[req, rows], out_sems.at[len(outs)])
            copy.start()
            outs.append(copy)
    loads[0].wait()
    wgrad[...] = dot_first(hist_ref[0], dk_ref[0])
    loads[1].wait()
    wgrad[...] += dot_first(hist_ref[1], dk_ref[1])
    put_shares(shares, wgrad)
    halve(shares, keep_ref, send_ref)
    for copy in outs:
        copy.wait()


def gather_kernel(part_ref, token_ref, dq_ref, att_ref):
    summed = jnp.sum(part_ref[...], axis=0)
    for dev in range(8):
        dq_ref[dev] = summed[0:16]
    for quarter in range(4):
        lanes = slice(128 * quarter, 128 * quarter + 128)
        att_ref[16 * quarter : 16 * quarter + 16] = summed[16:32, lanes]


def halves_kernel(keep_ref, recv_ref, token_ref, part0, part1, part2, part3):
    for slot, part in enumerate((part0, part1, part2, part3)):
        part[...] = keep_ref[slot] + recv_ref[slot]


def hist_grads_kernel(dk_hbm, dv_hbm, wk_hbm, wv_hbm, token_ref, out_hbm, done_ref,
                      dk_ref, dv_ref, wk_ref, wv_ref, buf, sems, out_sems):
    weights = [pltpu.make_async_copy(wk_hbm, wk_ref, sems.at[0]),
               pltpu.make_async_copy(wv_hbm, wv_ref, sems.at[1])]
    for copy in weights:
        copy.start()
    ins = []
    for req in range(2):
        for rows in tiles(buf):
            two = []
            for src, dst in ((dk_hbm, dk_ref), (dv_hbm, dv_ref)):
                copy = pltpu.make_async_copy(
                    src.at[req, rows], dst.at[req, rows], sems.at[2 + 2 * len(ins) + len(two)])
                copy.start()
                two.append(copy)
            ins.append(two)
    for copy in weights:
        copy.wait()
    copies = []
    for req in range(2):
        for rows in tiles(buf):
            for copy in ins[len(copies)]:
                copy.wait()
            buf[req, rows] = (dot_last(dk_ref[req, rows], wk_ref[...])
                              + dot_last(dv_ref[req, rows], wv_ref[...])).astype(BF16)
            copy = pltpu.make_async_copy(
                buf.at[req, rows], out_hbm.at[req, rows], out_sems.at[len(copies)])
            copy.start()
            copies.append(copy)
    done_ref[...] = jnp.zeros(done_ref.shape, F32)
    for copy in copies:
        copy.wait()


def outer_kernel(*refs):
    keys = refs[0:4]
    vals = refs[4:8]
    dq_ref, tok_ref, att_ref, dout_ref, token_ref, out_ref = refs[8:]
    dq = (dq_ref[...].reshape(128, 512) * 0.125).astype(BF16)
    row = lax.broadcasted_iota(jnp.int32, (64, 512), 0)
    col = lax.broadcasted_iota(jnp.int32, (64, 512), 1)
    feature = (row // 4) * 32 + lax.axis_index("seq") * 4 + row % 4
    pick = jnp.where(col == feature, 1.0, 0.0).astype(BF16)
    tok = dot_last(pick, tok_ref[...]).astype(BF16)
    parts = [dot(tok, dq),
             keys[0][...] + keys[1][...] + keys[2][...] + keys[3][...],
             vals[0][...] + vals[1][...] + vals[2][...] + vals[3][...],
             dot(att_ref[...].astype(BF16), dout_ref[...])]
    for dp in range(16):
        for part in range(4):
            out_ref[dp, 4 * part : 4 * part + 4] = parts[part][4 * dp : 4 * dp + 4]


def query_grad_kernel(dq_ref, wq_ref, token_ref, out_ref):
    dq = (dq_ref[...].reshape(128, 512) * 0.125).astype(BF16)
    out_ref[...] = dot_last(dq, wq_ref[...]).astype(BF16)


def final_kernel(part_ref, out_ref):
    summed = jnp.sum(part_ref[...], axis=0)
    for part in range(4):
        out_ref[:, part, :] = summed[4 * part : 4 * part + 4]


IN_VMEM = pl.BlockSpec(memory_space=VMEM)
IN_HBM = pl.BlockSpec(memory_space=pl.ANY)
IN_SMEM = pl.BlockSpec(memory_space=pltpu.MemorySpace.SMEM)


def call(kernel, args, outs, scratch=(), limit=26):
    specs = {"vmem": IN_VMEM, "hbm": IN_HBM, "smem": IN_SMEM}
    spaces = {"vmem": VMEM, "hbm": HBM}
    ins = [pltpu.with_memory_space_constraint(x, spaces[s]) if s in spaces else x for x, s in args]
    return pl.pallas_call(
        kernel,
        in_specs=[specs[s] for _, s in args],
        out_specs=[specs[s] for s, _, _ in outs],
        out_shape=[spaces[s](shape, dtype) for s, dtype, shape in outs],
        scratch_shapes=scratch,
        compiler_params=pltpu.CompilerParams(vmem_limit_bytes=limit * 1024 * 1024),
    )(*ins)


def swap(x, axis):
    return lax.all_to_all(x, axis, 0, 0)


def up(x, chips):
    return lax.ppermute(x, "seq", [(i, (i + 2 * chips) % 8) for i in range(8)])


def across(x):
    return lax.ppermute(x, "seq", [(i, i ^ 1) for i in range(8)])


def from_chips(x):
    return [x] + [up(x, chips) for chips in (1, 2, 3)]


def per_device(query_tokens, owner, d_out, history, lengths, w_query, w_key, w_value, w_out):
    rows, width = query_tokens.shape
    requests, events, _ = history.shape
    steps = events // TILE
    ev = (requests, events, width)
    mat = (width, width)
    blk = (PAIRS, 256, 256)
    vec = ("vmem", F32, (8, 256))
    pairs = (events, 256 * PAIRS)
    half = ("vmem", F32, (4, 64, width))
    quarter = ("vmem", F32, (64, width))
    dma = pltpu.SemaphoreType.DMA
    v = lambda *xs: [(x, "vmem") for x in xs]
    h = lambda *xs: [(x, "hbm") for x in xs]

    keys, hist, stats, lim, qb, own, qbt = call(
        keys_kernel,
        [(lengths, "smem")] + h(owner.reshape(1, rows), query_tokens, w_query, w_key, history),
        [("vmem", BF16, ev), ("vmem", BF16, ev), vec, ("vmem", jnp.int32, (8, 256)),
         ("vmem", BF16, blk), ("vmem", jnp.int32, (1, rows)), ("hbm", BF16, blk)],
        [pltpu.VMEM(blk, BF16), pltpu.VMEM((rows, width), BF16), pltpu.VMEM(mat, BF16),
         pltpu.VMEM(mat, BF16), dma((5 + 2 * steps,))],
    )
    stats = from_chips(stats)
    values, gb, gbt = call(
        values_kernel,
        h(w_value, d_out, w_out) + v(own, hist),
        [("vmem", BF16, ev), ("vmem", BF16, blk), ("vmem", BF16, blk)],
        [pltpu.VMEM(mat, BF16), pltpu.VMEM((rows, width), BF16), pltpu.VMEM(mat, BF16),
         dma((3,))],
    )
    stats = stats + [across(x) for x in stats]
    probs, delta = call(
        probs_kernel, v(*stats, lim, qb, gb, keys, values), [("vmem", BF16, pairs), vec])
    delta = from_chips(delta)
    dv, keep, send = call(
        value_grads_kernel, v(probs, hist, gbt), [("hbm", BF16, ev), half, half],
        [pltpu.VMEM(ev, BF16), pltpu.VMEM(mat, F32), pltpu.VMEM((8, 64, width), F32),
         dma((2 * steps,))])
    recv = across(send)
    delta = delta + [across(x) for x in delta]
    (att,) = call(
        attention_kernel, v(own, probs, values, keep), [("vmem", F32, (width, rows))])

    ds, part, *wgrad_v = call(
        query_part_kernel, v(*delta, own, probs, keys, values, gb, att, keep, recv),
        [("hbm", BF16, pairs), ("vmem", F32, (8, 32, width))] + [quarter] * 4,
        [pltpu.VMEM(pairs, BF16), dma((steps,))])
    part = swap(part, "seq")
    wgrad_v = [wgrad_v[0]] + [up(wgrad_v[i], i) for i in (1, 2, 3)]
    dk, keep, send = call(
        key_grads_kernel, h(ds, history, qbt), [("hbm", BF16, ev), half, half],
        [pltpu.VMEM(pairs, BF16), pltpu.VMEM(ev, BF16), pltpu.VMEM(blk, BF16),
         pltpu.VMEM(ev, BF16), pltpu.VMEM(mat, F32), pltpu.VMEM((8, 64, width), F32),
         dma((3 + steps,)), dma((2 * steps,))])
    recv = across(send)
    dq, att = call(
        gather_kernel, v(part) + h(dk),
        [("vmem", F32, (8, 16, width)), ("vmem", F32, (64, rows))])
    wgrad_k = call(halves_kernel, v(keep, recv, att), [quarter] * 4)
    dq = swap(dq, "seq")
    token = wgrad_k[0]
    wgrad_k = [wgrad_k[0]] + [up(wgrad_k[i], i) for i in (1, 2, 3)]
    hist_grad, token = call(
        hist_grads_kernel, h(dk, dv, w_key, w_value) + v(token),
        [("hbm", BF16, ev), ("vmem", F32, (8, 128))],
        [pltpu.VMEM(ev, BF16), pltpu.VMEM(ev, BF16), pltpu.VMEM(mat, BF16),
         pltpu.VMEM(mat, BF16), pltpu.VMEM(ev, BF16), dma((2 + 4 * steps,)), dma((2 * steps,))])
    (outer,) = call(
        outer_kernel, v(*wgrad_k, *wgrad_v, dq, query_tokens, att, d_out, token),
        [("vmem", F32, (16, 16, width))])
    token = outer
    outer = swap(outer, "dp")
    (query_grad,) = call(
        query_grad_kernel, v(dq, w_query, token), [("vmem", BF16, (rows, width))])
    (weight_part,) = call(final_kernel, v(outer), [("vmem", F32, (4, 4, width))])
    return query_grad, hist_grad, weight_part


def solution(mesh):
    return jax.shard_map(
        per_device,
        mesh=mesh,
        in_specs=(
            P("dp", None),
            P("dp"),
            P("dp", None),
            P("dp", "seq", None),
            P("dp"),
            P(),
            P(),
            P(),
            P(),
        ),
        out_specs=(P("dp", None), P("dp", "seq", None), P(("dp", "seq"), None, None)),
        check_vma=False,
    )
```

```python
import jax
import jax.numpy as jnp
from jax import lax
from jax.experimental import pallas as pl
from jax.experimental.pallas import tpu as pltpu
from jax.sharding import PartitionSpec as P

PAIRS = 4
LOW = -1e30
F32 = jnp.float32
BF16 = jnp.bfloat16
VMEM = pltpu.MemorySpace.VMEM
HBM = pltpu.MemorySpace.HBM
TILE = 1024


def dot(left, right):
    return jnp.dot(left, right, preferred_element_type=F32)


def dot_last(left, right):
    return lax.dot_general(left, right, (((1,), (1,)), ((), ())), preferred_element_type=F32)


def dot_first(left, right):
    return lax.dot_general(left, right, (((0,), (0,)), ((), ())), preferred_element_type=F32)


def tiles(ref):
    events = ref.shape[1]
    return [slice(start, start + TILE) for start in range(0, events, TILE)]


def pair_cols(ref, pair, rows):
    cols = slice(128 * pair, 128 * pair + 128)
    return jnp.concatenate([ref[0, rows, cols], ref[1, rows, cols]], axis=1)


def put_pair(ref, pair, rows, value):
    cols = slice(128 * pair, 128 * pair + 128)
    ref[0, rows, cols] = value[:, 0:128]
    ref[1, rows, cols] = value[:, 128:256]


def pair_lanes(pair):
    return slice(256 * pair, 256 * pair + 256)


def seen_in(lim_ref, rows):
    place = lax.broadcasted_iota(jnp.int32, (TILE, 256), 0) + rows.start
    return place < lim_ref[0:1]


def spread(full, own_col, owner_row, blk_ref, blk_t_ref):
    lane = lax.broadcasted_iota(jnp.int32, (128, 128), 1)
    zero = jnp.zeros((64, 128), F32)
    for pair in range(PAIRS):
        part = full[:, 128 * pair : 128 * pair + 128]
        part_t = part.T
        for req in range(2):
            mine = jnp.where(own_col == req, part, 0.0)
            cols = slice(128 * req, 128 * req + 128)
            blk_t_ref[pair, 0:128, cols] = jnp.where(lane < 64, mine, 0.0).astype(BF16)
            blk_t_ref[pair, 128:256, cols] = jnp.where(lane < 64, 0.0, mine).astype(BF16)
            mine_t = jnp.where(owner_row == req, part_t, 0.0)
            top = jnp.concatenate([mine_t[0:64], zero], axis=1)
            low = jnp.concatenate([zero, mine_t[64:128]], axis=1)
            blk_ref[pair, cols, :] = jnp.concatenate([top, low], axis=0).astype(BF16)


def keys_kernel(lens_hbm, own_hbm, tok_hbm, wq_hbm, wk_hbm, hist_hbm,
                key_ref, hist_ref, stat_ref, lim_ref, qb_ref, own_ref, qbt_ref,
                lens_ref, tok_ref, wq_ref, wk_ref, sems):
    small = [(wq_hbm, wq_ref), (tok_hbm, tok_ref), (own_hbm, own_ref), (lens_hbm, lens_ref),
             (wk_hbm, wk_ref)]
    small = [pltpu.make_async_copy(src, dst, sems.at[i]) for i, (src, dst) in enumerate(small)]
    for copy in small:
        copy.start()
    chunks = []
    for rows in tiles(hist_ref):
        for req in range(2):
            copy = pltpu.make_async_copy(
                hist_hbm.at[req, rows], hist_ref.at[req, rows], sems.at[5 + len(chunks)])
            copy.start()
            chunks.append(copy)
    for copy in small[0:4]:
        copy.wait()
    owner_row = jnp.broadcast_to(own_ref[...], (128, 128))
    base = lax.axis_index("seq") * hist_ref.shape[1]
    lim = jnp.where(own_ref[...] == 0, lens_ref[0], lens_ref[1]) - base
    lim_ref[...] = jnp.broadcast_to(jnp.concatenate([lim, lim], axis=1), (8, 256))
    q = dot(tok_ref[...], wq_ref[...]).astype(BF16).astype(F32) * 0.125
    spread(q, owner_row.T, owner_row[0:1], qb_ref, qbt_ref)
    small[4].wait()
    for index, rows in enumerate(tiles(hist_ref)):
        for req in range(2):
            chunks[2 * index + req].wait()
            key_ref[req, rows] = dot(hist_ref[req, rows], wk_ref[...]).astype(BF16)
    tops, sums = [], []
    for pair in range(PAIRS):
        tops.append([])
        sums.append([])
    for rows in tiles(hist_ref):
        seen = seen_in(lim_ref, rows)
        for pair in range(PAIRS):
            score = jnp.where(seen, dot(pair_cols(key_ref, pair, rows), qb_ref[pair]), LOW)
            top = jnp.max(score, axis=0, keepdims=True)
            tops[pair].append(top)
            sums[pair].append(jnp.sum(jnp.exp(score - top), axis=0, keepdims=True))
    peaks, totals = [], []
    for pair in range(PAIRS):
        peak = tops[pair][0]
        for top in tops[pair][1:]:
            peak = jnp.maximum(peak, top)
        peaks.append(peak)
        totals.append(sum(x * jnp.exp(top - peak) for x, top in zip(sums[pair], tops[pair])))
    stat_ref[...] = jnp.concatenate(peaks + totals, axis=0)


def values_kernel(wv_ref, hist_ref, val_ref):
    for rows in tiles(hist_ref):
        for req in range(2):
            val_ref[req, rows] = dot(hist_ref[req, rows], wv_ref[...]).astype(BF16)


def join_stats_kernel(*refs):
    stats, out_ref = refs[0:4], refs[-1]
    top = stats[0][0:4]
    for stat in stats[1:]:
        top = jnp.maximum(top, stat[0:4])
    norm = jnp.zeros((4, 256), F32)
    for stat in stats:
        norm += stat[4:8] * jnp.exp(stat[0:4] - top)
    out_ref[...] = jnp.concatenate([top, norm], axis=0)


def join_deltas_kernel(*refs):
    refs[-1][...] = refs[0][...] + refs[1][...] + refs[2][...] + refs[3][...]


def out_grads_kernel(dout_ref, wout_ref, own_ref, token_ref, gb_ref, gbt_ref):
    owner_row = jnp.broadcast_to(own_ref[...], (128, 128))
    g = dot_last(dout_ref[...], wout_ref[...]).astype(BF16).astype(F32)
    spread(g, owner_row.T, owner_row[0:1], gb_ref, gbt_ref)


def probs_kernel(one_ref, two_ref, lim_ref, qb_ref, gb_ref, key_ref, val_ref, prob_ref, delta_ref):
    one, two = one_ref[0:4], two_ref[0:4]
    top = jnp.maximum(one, two)
    norm = one_ref[4:8] * jnp.exp(one - top) + two_ref[4:8] * jnp.exp(two - top)
    shift = top + jnp.log(norm)
    delta = [jnp.zeros((1, 256), F32) for _ in range(PAIRS)]
    for rows in tiles(key_ref):
        seen = seen_in(lim_ref, rows)
        for pair in range(PAIRS):
            score = dot(pair_cols(key_ref, pair, rows), qb_ref[pair])
            prob = jnp.where(seen, jnp.exp(score - shift[pair : pair + 1]), 0.0).astype(BF16)
            prob_ref[rows, pair_lanes(pair)] = prob
            slope = dot(pair_cols(val_ref, pair, rows), gb_ref[pair])
            delta[pair] += jnp.sum(prob.astype(F32) * slope, axis=0, keepdims=True)
    delta_ref[...] = jnp.concatenate(delta + [jnp.zeros((4, 256), F32)], axis=0)


def put_shares(out_ref, value):
    for row in range(0, 512, 4):
        dp, seq = row // 32, (row // 4) % 8
        out_ref[seq, 4 * dp : 4 * dp + 4] = value[row : row + 4]


def put_shares(out_ref, value):
    for row in range(0, 512, 4):
        dp, seq = row // 32, (row // 4) % 8
        out_ref[seq, 4 * dp : 4 * dp + 4] = value[row : row + 4]


def halve(shares, keep_ref, send_ref, rows):
    me = lax.axis_index("seq")
    for slot in range(4):
        chip = lax.rem(me // 2 + slot, 4)
        keep_ref[slot, rows] = shares[2 * chip + lax.rem(me, 2)]
        send_ref[slot, rows] = shares[2 * chip + 1 - lax.rem(me, 2)]


def value_grads_kernel(prob_ref, hist_ref, gbt_ref, dv_ref, share_ref, wgrad):
    for rows in tiles(hist_ref):
        for pair in range(PAIRS):
            grad = dot(prob_ref[rows, pair_lanes(pair)], gbt_ref[pair]).astype(BF16)
            put_pair(dv_ref, pair, rows, grad)
    wgrad[...] = dot_first(hist_ref[0], dv_ref[0])
    wgrad[...] += dot_first(hist_ref[1], dv_ref[1])
    put_shares(share_ref, wgrad)


def attention_kernel(own_ref, prob_ref, val_ref, token_ref, att_ref):
    first = own_ref[...] == 0
    for pair in range(PAIRS):
        blk = jnp.zeros((256, 256), F32)
        for rows in tiles(val_ref):
            blk += dot_first(pair_cols(val_ref, pair, rows), prob_ref[rows, pair_lanes(pair)])
        for head in range(2):
            lanes = slice(128 * head, 128 * head + 128)
            one = blk[64 * head : 64 * head + 64, lanes]
            two = blk[128 + 64 * head : 192 + 64 * head, lanes]
            out = jnp.where(first, one, two)
            for row in range(0, 64, 4):
                feature = 128 * pair + 64 * head + row
                dp, seq = feature // 32, (feature // 4) % 8
                start = 4 * (dp % 4)
                att_ref[seq, start : start + 4, 128 * (dp // 4) : 128 * (dp // 4) + 128] = (
                    out[row : row + 4])


def query_part_kernel(one_ref, two_ref, own_ref, prob_ref, key_ref, val_ref, gb_ref, att_ref,
                      share_ref, ds_ref, keep_ref, send_ref, dq_ref):
    delta = one_ref[...] + two_ref[...]
    own_col = jnp.broadcast_to(own_ref[...], (128, 128)).T
    lane = lax.broadcasted_iota(jnp.int32, (128, 128), 1)
    blks = [jnp.zeros((256, 256), F32) for _ in range(PAIRS)]
    for rows in tiles(key_ref):
        for pair in range(PAIRS):
            prob = prob_ref[rows, pair_lanes(pair)].astype(F32)
            slope = dot(pair_cols(val_ref, pair, rows), gb_ref[pair])
            ds = (prob * (slope - delta[pair : pair + 1])).astype(BF16)
            ds_ref[rows, pair_lanes(pair)] = ds
            blks[pair] += dot_first(ds, pair_cols(key_ref, pair, rows))
    for pair in range(PAIRS):
        blk = blks[pair]
        one = jnp.where(own_col == 0, blk[:128, :128], blk[:128, 128:])
        two = jnp.where(own_col == 0, blk[128:, :128], blk[128:, 128:])
        dq = jnp.where(lane < 64, one, two)
        for dev in range(8):
            dq_ref[dev, :, 128 * pair : 128 * pair + 128] = dq[16 * dev : 16 * dev + 16]
    halve(share_ref, keep_ref, send_ref, slice(0, 64))
    halve(dq_ref, keep_ref, send_ref, slice(64, 80))
    halve(att_ref, keep_ref, send_ref, slice(80, 96))


def key_grads_kernel(ds_ref, qbt_ref, dk_ref):
    for rows in tiles(dk_ref):
        for pair in range(PAIRS):
            grad = dot(ds_ref[rows, pair_lanes(pair)], qbt_ref[pair]).astype(BF16)
            put_pair(dk_ref, pair, rows, grad)


def key_weight_kernel(hist_ref, dk_ref, token_ref, keep_ref, send_ref, wgrad, shares):
    wgrad[...] = dot_first(hist_ref[0], dk_ref[0])
    wgrad[...] += dot_first(hist_ref[1], dk_ref[1])
    put_shares(shares, wgrad)
    halve(shares, keep_ref, send_ref, slice(0, 64))


def join_halves_kernel(keep_ref, recv_ref, token_ref, *parts):
    for slot, part in enumerate(parts):
        part[...] = keep_ref[slot] + recv_ref[slot]


def gather_kernel(part0, part1, part2, part3, send_ref, wv_ref, dq_ref, att_ref, same_ref):
    summed = part0[...] + part1[...] + part2[...] + part3[...]
    wv_ref[...] = summed[0:64]
    dq_ref[...] = summed[64:80]
    for quarter in range(4):
        lanes = slice(128 * quarter, 128 * quarter + 128)
        att_ref[16 * quarter : 16 * quarter + 16] = summed[80:96, lanes]


def join_keys_kernel(keep_ref, recv_ref, mine_ref, other_ref, *parts):
    even = lax.rem(lax.axis_index("seq"), 2) == 0
    mine, other = mine_ref[...], other_ref[...]
    for slot, part in enumerate(parts):
        part[0:64] = keep_ref[slot] + recv_ref[slot]
        part[64:80] = jnp.where(even, mine, other)
        part[80:96] = jnp.where(even, other, mine)


def hist_grads(req, dk_ref, dv_ref, wk_ref, wv_ref, out_hbm, done_ref, buf, sems):
    copies = []
    for start in range(0, buf.shape[0], 512):
        rows = slice(start, start + 512)
        buf[rows] = (dot_last(dk_ref[req, rows], wk_ref[...])
                     + dot_last(dv_ref[req, rows], wv_ref[...])).astype(BF16)
        copy = pltpu.make_async_copy(buf.at[rows], out_hbm.at[req, rows], sems.at[len(copies)])
        copy.start()
        copies.append(copy)
    done_ref[...] = jnp.zeros(done_ref.shape, F32)
    for copy in copies:
        copy.wait()


def hist_grads_first_kernel(dk_ref, dv_ref, wk_ref, wv_ref, token_ref, *refs):
    hist_grads(0, dk_ref, dv_ref, wk_ref, wv_ref, *refs)


def hist_grads_second_kernel(dk_ref, dv_ref, wk_ref, wv_ref, token_ref, in_hbm, *refs):
    hist_grads(1, dk_ref, dv_ref, wk_ref, wv_ref, *refs)


def outer_kernel(*refs):
    keys = refs[0:4]
    wv_ref, tok_ref, att_ref, dout_ref, token_ref = refs[4:9]
    outs, (low_ref, dq_ref, all_ref) = refs[9:13], refs[13:]
    me = lax.axis_index("seq")
    for chips, part in enumerate(keys):
        dq_ref[lax.rem(me // 2 + 4 - chips, 4)] = part[64:96]
    dq = (dq_ref[...].reshape(128, 512) * 0.125).astype(BF16)
    low_ref[...] = dq
    row = lax.broadcasted_iota(jnp.int32, (64, 512), 0)
    col = lax.broadcasted_iota(jnp.int32, (64, 512), 1)
    feature = (row // 4) * 32 + me * 4 + row % 4
    pick = jnp.where(col == feature, 1.0, 0.0).astype(BF16)
    tok = dot_last(pick, tok_ref[...]).astype(BF16)
    parts = [dot(tok, dq),
             keys[0][0:64] + keys[1][0:64] + keys[2][0:64] + keys[3][0:64],
             wv_ref[...],
             dot(att_ref[...].astype(BF16), dout_ref[...])]
    for dp in range(16):
        for part in range(4):
            all_ref[dp, 4 * part : 4 * part + 4] = parts[part][4 * dp : 4 * dp + 4]
    y = lax.axis_index("dp") // 4
    for chips, out in enumerate(outs):
        out[...] = all_ref[pl.ds(4 * lax.rem(y + chips, 4), 4)]


def join_y_kernel(*refs):
    parts, outs, (sum_ref,) = refs[0:4], refs[5:9], refs[9:]
    sum_ref[...] = parts[0][...] + parts[1][...] + parts[2][...] + parts[3][...]
    x = lax.rem(lax.axis_index("dp"), 4)
    for chips, out in enumerate(outs):
        out[...] = sum_ref[lax.rem(x + chips, 4)]


def query_grad_kernel(dq_ref, wq_ref, out_ref):
    out_ref[...] = dot_last(dq_ref[...], wq_ref[...]).astype(BF16)


def final_kernel(part0, part1, part2, part3, out_ref):
    summed = part0[...] + part1[...] + part2[...] + part3[...]
    for part in range(4):
        out_ref[:, part, :] = summed[4 * part : 4 * part + 4]


IN_VMEM = pl.BlockSpec(memory_space=VMEM)
IN_HBM = pl.BlockSpec(memory_space=pl.ANY)


def call(kernel, args, outs, scratch=(), aliases=(), limit=26):
    specs = {"vmem": IN_VMEM, "hbm": IN_HBM}
    spaces = {"vmem": VMEM, "hbm": HBM}
    ins = [pltpu.with_memory_space_constraint(x, spaces[s]) for x, s in args]
    return pl.pallas_call(
        kernel,
        in_specs=[specs[s] for _, s in args],
        out_specs=[specs[s] for s, _, _ in outs],
        out_shape=[spaces[s](shape, dtype) for s, dtype, shape in outs],
        scratch_shapes=scratch,
        input_output_aliases=dict(aliases),
        compiler_params=pltpu.CompilerParams(vmem_limit_bytes=limit * 1024 * 1024),
    )(*ins)


def turn(x, to):
    return lax.ppermute(x, "dp", [(i, to(i // 4, i % 4)) for i in range(16)])


def up(x, chips):
    return lax.ppermute(x, "seq", [(i, (i + 2 * chips) % 8) for i in range(8)])


def across(x):
    return lax.ppermute(x, "seq", [(i, i ^ 1) for i in range(8)])


def from_chips(x):
    return [x] + [up(x, chips) for chips in (1, 2, 3)]


def per_device(query_tokens, owner, d_out, history, lengths, w_query, w_key, w_value, w_out):
    rows, width = query_tokens.shape
    requests, events, _ = history.shape
    steps = events // TILE
    ev = (requests, events, width)
    mat = (width, width)
    blk = (PAIRS, 256, 256)
    vec = ("vmem", F32, (8, 256))
    pairs = (events, 256 * PAIRS)
    half = ("vmem", F32, (4, 64, width))
    quarter = ("vmem", F32, (64, width))
    wide_half = ("vmem", F32, (4, 96, width))
    wide = ("vmem", F32, (96, width))
    dma = pltpu.SemaphoreType.DMA
    v = lambda *xs: [(x, "vmem") for x in xs]
    h = lambda *xs: [(x, "hbm") for x in xs]

    keys, hist, stats, lim, qb, own, qbt = call(
        keys_kernel,
        h(lengths, owner.reshape(1, rows), query_tokens, w_query, w_key, history),
        [("vmem", BF16, ev), ("vmem", BF16, ev), vec, ("vmem", jnp.int32, (8, 256)),
         ("vmem", BF16, blk), ("vmem", jnp.int32, (1, rows)), ("vmem", BF16, blk)],
        [pltpu.SMEM((requests,), jnp.int32), pltpu.VMEM((rows, width), BF16),
         pltpu.VMEM(mat, BF16), pltpu.VMEM(mat, BF16), dma((5 + 2 * steps,))],
    )
    stats = from_chips(stats)
    (values,) = call(values_kernel, v(w_value, hist), [("vmem", BF16, ev)])
    (stats,) = call(join_stats_kernel, v(*stats, values), [vec])
    gb, gbt = call(
        out_grads_kernel, v(d_out, w_out, own, stats), [("vmem", BF16, blk), ("vmem", BF16, blk)])
    probs, delta = call(
        probs_kernel, v(stats, across(stats), lim, qb, gb, keys, values),
        [("vmem", BF16, pairs), vec])
    delta = from_chips(delta)
    dv, share = call(
        value_grads_kernel, v(probs, hist, gbt), [("vmem", BF16, ev), ("vmem", F32, (8, 64, width))],
        [pltpu.VMEM(mat, F32)])
    (delta,) = call(join_deltas_kernel, v(*delta, dv), [vec])
    (att,) = call(
        attention_kernel, v(own, probs, values, delta), [("vmem", F32, (8, 16, width))])

    ds, keep, send = call(
        query_part_kernel, v(delta, across(delta), own, probs, keys, values, gb, att, share),
        [("vmem", BF16, pairs), wide_half, wide_half], [pltpu.VMEM((8, 16, width), F32)])
    (dk,) = call(key_grads_kernel, v(ds, qbt), [("vmem", BF16, ev)])
    parts = call(join_halves_kernel, v(keep, across(send), dk), [wide] * 4)
    token = parts[0]
    parts = [parts[0]] + [up(parts[i], i) for i in (1, 2, 3)]
    keep, send = call(
        key_weight_kernel, v(hist, dk, token), [half, half],
        [pltpu.VMEM(mat, F32), pltpu.VMEM((8, 64, width), F32)])
    wgrad_v, dq, att, send = call(
        gather_kernel, v(*parts, send),
        [quarter, ("vmem", F32, (16, width)), ("vmem", F32, (64, rows)), half], aliases={4: 3})
    parts = call(join_keys_kernel, v(keep, across(send), dq, across(dq)), [wide] * 4)
    token = parts[0]
    parts = [parts[0]] + [up(parts[i], i) for i in (1, 2, 3)]
    grad_out = [("hbm", BF16, ev), ("vmem", F32, (8, 128))]
    grad_scratch = [pltpu.VMEM((events, width), BF16), dma((events // 512,))]
    hist_grad, token = call(
        hist_grads_first_kernel, v(dk, dv, w_key, w_value, token), grad_out, grad_scratch)
    *outer, dq = call(
        outer_kernel, v(*parts, wgrad_v, query_tokens, att, d_out, token),
        [("vmem", F32, (4, 16, width))] * 4 + [("vmem", BF16, (rows, width))],
        [pltpu.VMEM((4, 32, width), F32), pltpu.VMEM((16, 16, width), F32)])
    outer = [outer[0]] + [turn(outer[i], lambda y, x: (y + i) % 4 * 4 + x) for i in (1, 2, 3)]
    hist_grad, token = call(
        hist_grads_second_kernel, v(dk, dv, w_key, w_value, dq) + h(hist_grad), grad_out,
        grad_scratch, aliases={5: 0})
    outer = call(
        join_y_kernel, v(*outer, token), [("vmem", F32, (16, width))] * 4,
        [pltpu.VMEM((4, 16, width), F32)])
    outer = [outer[0]] + [turn(outer[i], lambda y, x: y * 4 + (x + i) % 4) for i in (1, 2, 3)]
    (query_grad,) = call(
        query_grad_kernel, v(dq, w_query), [("vmem", BF16, (rows, width))])
    (weight_part,) = call(final_kernel, v(*outer), [("vmem", F32, (4, 4, width))])
    return query_grad, hist_grad, weight_part


def solution(mesh):
    return jax.shard_map(
        per_device,
        mesh=mesh,
        in_specs=(
            P("dp", None),
            P("dp"),
            P("dp", None),
            P("dp", "seq", None),
            P("dp"),
            P(),
            P(),
            P(),
            P(),
        ),
        out_specs=(P("dp", None), P("dp", "seq", None), P(("dp", "seq"), None, None)),
        check_vma=False,
    )
```

```python
import jax
import jax.numpy as jnp
from jax import lax
from jax.experimental import pallas as pl
from jax.experimental.pallas import tpu as pltpu
from jax.sharding import PartitionSpec as P

PAIRS = 4
LOW = -1e30
F32 = jnp.float32
BF16 = jnp.bfloat16
VMEM = pltpu.MemorySpace.VMEM
HBM = pltpu.MemorySpace.HBM
TILE = 1024
LIMIT = 8


def dot(left, right):
    return jnp.dot(left, right, preferred_element_type=F32)


def dot_last(left, right):
    return lax.dot_general(left, right, (((1,), (1,)), ((), ())), preferred_element_type=F32)


def dot_first(left, right):
    return lax.dot_general(left, right, (((0,), (0,)), ((), ())), preferred_element_type=F32)


def tiles(ref):
    events = ref.shape[1]
    return [slice(start, start + TILE) for start in range(0, events, TILE)]


def pair_cols(ref, pair, rows):
    cols = slice(128 * pair, 128 * pair + 128)
    return jnp.concatenate([ref[0, rows, cols], ref[1, rows, cols]], axis=1)


def put_pair(ref, pair, rows, value):
    cols = slice(128 * pair, 128 * pair + 128)
    ref[0, rows, cols] = value[:, 0:128]
    ref[1, rows, cols] = value[:, 128:256]


def pair_lanes(pair):
    return slice(256 * pair, 256 * pair + 256)


def seen_in(lim_ref, rows):
    place = lax.broadcasted_iota(jnp.int32, (TILE, 256), 0) + rows.start
    return place < lim_ref[0:1]


def spread(full, own_col, owner_row, blk_ref, blk_t_ref):
    lane = lax.broadcasted_iota(jnp.int32, (128, 128), 1)
    zero = jnp.zeros((64, 128), F32)
    for pair in range(PAIRS):
        part = full[:, 128 * pair : 128 * pair + 128]
        part_t = part.T
        for req in range(2):
            mine = jnp.where(own_col == req, part, 0.0)
            cols = slice(128 * req, 128 * req + 128)
            blk_t_ref[pair, 0:128, cols] = jnp.where(lane < 64, mine, 0.0).astype(BF16)
            blk_t_ref[pair, 128:256, cols] = jnp.where(lane < 64, 0.0, mine).astype(BF16)
            mine_t = jnp.where(owner_row == req, part_t, 0.0)
            top = jnp.concatenate([mine_t[0:64], zero], axis=1)
            low = jnp.concatenate([zero, mine_t[64:128]], axis=1)
            blk_ref[pair, cols, :] = jnp.concatenate([top, low], axis=0).astype(BF16)


def keys_kernel(lens_hbm, own_hbm, tok_hbm, wq_hbm, wk_hbm, hist_hbm,
                key_ref, hist_ref, stat_ref, expo_ref, top_ref, own_ref, qbt_ref,
                lens_ref, lim_ref, qb_ref, tok_ref, wq_ref, wk_ref, sems):
    small = [(wq_hbm, wq_ref), (tok_hbm, tok_ref), (own_hbm, own_ref), (lens_hbm, lens_ref),
             (wk_hbm, wk_ref)]
    small = [pltpu.make_async_copy(src, dst, sems.at[i]) for i, (src, dst) in enumerate(small)]
    for copy in small:
        copy.start()
    chunks = []
    for rows in tiles(hist_ref):
        for req in range(2):
            copy = pltpu.make_async_copy(
                hist_hbm.at[req, rows], hist_ref.at[req, rows], sems.at[5 + len(chunks)])
            copy.start()
            chunks.append(copy)
    for copy in small[0:4]:
        copy.wait()
    owner_row = jnp.broadcast_to(own_ref[...], (128, 128))
    base = lax.axis_index("seq") * hist_ref.shape[1]
    lim = jnp.where(own_ref[...] == 0, lens_ref[0], lens_ref[1]) - base
    lim_ref[...] = jnp.broadcast_to(jnp.concatenate([lim, lim], axis=1), (8, 256))
    q = dot(tok_ref[...], wq_ref[...]).astype(BF16).astype(F32) * 0.125
    spread(q, owner_row.T, owner_row[0:1], qb_ref, qbt_ref)
    small[4].wait()
    for index, rows in enumerate(tiles(hist_ref)):
        for req in range(2):
            chunks[2 * index + req].wait()
            key_ref[req, rows] = dot(hist_ref[req, rows], wk_ref[...]).astype(BF16)
    tops, sums = [], []
    for pair in range(PAIRS):
        tops.append([])
        sums.append([])
    for rows in tiles(hist_ref):
        seen = seen_in(lim_ref, rows)
        for pair in range(PAIRS):
            score = jnp.where(seen, dot(pair_cols(key_ref, pair, rows), qb_ref[pair]), LOW)
            top = jnp.max(score, axis=0, keepdims=True)
            tops[pair].append(top)
            expo = jnp.exp(score - top)
            expo_ref[rows, pair_lanes(pair)] = expo
            sums[pair].append(jnp.sum(expo, axis=0, keepdims=True))
    peaks, totals = [], []
    for pair in range(PAIRS):
        peak = tops[pair][0]
        for top in tops[pair][1:]:
            peak = jnp.maximum(peak, top)
        peaks.append(peak)
        totals.append(sum(x * jnp.exp(top - peak) for x, top in zip(sums[pair], tops[pair])))
    stat_ref[...] = jnp.concatenate(peaks + totals, axis=0)
    for pair in range(PAIRS):
        for index, top in enumerate(tops[pair]):
            top_ref[index, pair : pair + 1] = top


def values_kernel(wv_ref, hist_ref, val_ref):
    for rows in tiles(hist_ref):
        for req in range(2):
            val_ref[req, rows] = dot(hist_ref[req, rows], wv_ref[...]).astype(BF16)


def join_stats_kernel(*refs):
    stats, out_ref = refs[0:4], refs[-1]
    top = stats[0][0:4]
    for stat in stats[1:]:
        top = jnp.maximum(top, stat[0:4])
    norm = jnp.zeros((4, 256), F32)
    for stat in stats:
        norm += stat[4:8] * jnp.exp(stat[0:4] - top)
    out_ref[...] = jnp.concatenate([top, norm], axis=0)


def join_deltas_kernel(*refs):
    refs[-1][...] = refs[0][...] + refs[1][...] + refs[2][...] + refs[3][...]


def out_grads_kernel(dout_ref, wout_ref, own_ref, token_ref, gb_ref, gbt_ref):
    owner_row = jnp.broadcast_to(own_ref[...], (128, 128))
    g = dot_last(dout_ref[...], wout_ref[...]).astype(BF16).astype(F32)
    spread(g, owner_row.T, owner_row[0:1], gb_ref, gbt_ref)


def probs_kernel(one_ref, two_ref, expo_ref, top_ref, gb_ref, val_ref, prob_ref, slope_ref, delta_ref):
    one, two = one_ref[0:4], two_ref[0:4]
    top = jnp.maximum(one, two)
    norm = one_ref[4:8] * jnp.exp(one - top) + two_ref[4:8] * jnp.exp(two - top)
    shift = top + jnp.log(norm)
    delta = [jnp.zeros((1, 256), F32) for _ in range(PAIRS)]
    for index, rows in enumerate(tiles(val_ref)):
        factor = jnp.exp(top_ref[index] - shift)
        for pair in range(PAIRS):
            lanes = pair_lanes(pair)
            prob = (expo_ref[rows, lanes] * factor[pair : pair + 1]).astype(BF16)
            prob_ref[rows, lanes] = prob
            slope = dot(pair_cols(val_ref, pair, rows), gb_ref[pair])
            slope_ref[rows, lanes] = slope
            delta[pair] += jnp.sum(prob.astype(F32) * slope, axis=0, keepdims=True)
    delta_ref[...] = jnp.concatenate(delta + [jnp.zeros((4, 256), F32)], axis=0)


def put_shares(out_ref, value):
    for row in range(0, 512, 4):
        dp, seq = row // 32, (row // 4) % 8
        out_ref[seq, 4 * dp : 4 * dp + 4] = value[row : row + 4]


def put_shares(out_ref, value):
    for row in range(0, 512, 4):
        dp, seq = row // 32, (row // 4) % 8
        out_ref[seq, 4 * dp : 4 * dp + 4] = value[row : row + 4]


def halve(shares, keep_ref, send_ref, rows):
    me = lax.axis_index("seq")
    for slot in range(4):
        chip = lax.rem(me // 2 + slot, 4)
        keep_ref[slot, rows] = shares[2 * chip + lax.rem(me, 2)]
        send_ref[slot, rows] = shares[2 * chip + 1 - lax.rem(me, 2)]


def value_grads_kernel(prob_ref, hist_ref, gbt_ref, dv_ref, share_ref, wgrad):
    for rows in tiles(hist_ref):
        for pair in range(PAIRS):
            grad = dot(prob_ref[rows, pair_lanes(pair)], gbt_ref[pair]).astype(BF16)
            put_pair(dv_ref, pair, rows, grad)
    wgrad[...] = dot_first(hist_ref[0], dv_ref[0])
    wgrad[...] += dot_first(hist_ref[1], dv_ref[1])
    put_shares(share_ref, wgrad)


def attention_kernel(own_ref, prob_ref, val_ref, token_ref, att_ref):
    first = own_ref[...] == 0
    for pair in range(PAIRS):
        blk = jnp.zeros((256, 256), F32)
        for rows in tiles(val_ref):
            blk += dot_first(pair_cols(val_ref, pair, rows), prob_ref[rows, pair_lanes(pair)])
        for head in range(2):
            lanes = slice(128 * head, 128 * head + 128)
            one = blk[64 * head : 64 * head + 64, lanes]
            two = blk[128 + 64 * head : 192 + 64 * head, lanes]
            out = jnp.where(first, one, two)
            for row in range(0, 64, 4):
                feature = 128 * pair + 64 * head + row
                dp, seq = feature // 32, (feature // 4) % 8
                start = 4 * (dp % 4)
                att_ref[seq, start : start + 4, 128 * (dp // 4) : 128 * (dp // 4) + 128] = (
                    out[row : row + 4])


def query_part_kernel(one_ref, two_ref, own_ref, prob_ref, key_ref, slope_ref, att_ref,
                      share_ref, ds_ref, keep_ref, send_ref, dq_ref):
    delta = one_ref[...] + two_ref[...]
    own_col = jnp.broadcast_to(own_ref[...], (128, 128)).T
    lane = lax.broadcasted_iota(jnp.int32, (128, 128), 1)
    blks = [jnp.zeros((256, 256), F32) for _ in range(PAIRS)]
    for rows in tiles(key_ref):
        for pair in range(PAIRS):
            prob = prob_ref[rows, pair_lanes(pair)].astype(F32)
            slope = slope_ref[rows, pair_lanes(pair)]
            ds = (prob * (slope - delta[pair : pair + 1])).astype(BF16)
            ds_ref[rows, pair_lanes(pair)] = ds
            blks[pair] += dot_first(ds, pair_cols(key_ref, pair, rows))
    for pair in range(PAIRS):
        blk = blks[pair]
        one = jnp.where(own_col == 0, blk[:128, :128], blk[:128, 128:])
        two = jnp.where(own_col == 0, blk[128:, :128], blk[128:, 128:])
        dq = jnp.where(lane < 64, one, two)
        for dev in range(8):
            dq_ref[dev, :, 128 * pair : 128 * pair + 128] = dq[16 * dev : 16 * dev + 16]
    halve(share_ref, keep_ref, send_ref, slice(0, 64))
    halve(dq_ref, keep_ref, send_ref, slice(64, 80))
    halve(att_ref, keep_ref, send_ref, slice(80, 96))


def key_grads_kernel(ds_ref, qbt_ref, dk_ref):
    for rows in tiles(dk_ref):
        for pair in range(PAIRS):
            grad = dot(ds_ref[rows, pair_lanes(pair)], qbt_ref[pair]).astype(BF16)
            put_pair(dk_ref, pair, rows, grad)


def key_weight_kernel(hist_ref, dk_ref, token_ref, keep_ref, send_ref, wgrad, shares):
    wgrad[...] = dot_first(hist_ref[0], dk_ref[0])
    wgrad[...] += dot_first(hist_ref[1], dk_ref[1])
    put_shares(shares, wgrad)
    halve(shares, keep_ref, send_ref, slice(0, 64))


def join_halves_kernel(keep_ref, recv_ref, token_ref, *parts):
    for slot, part in enumerate(parts):
        part[...] = keep_ref[slot] + recv_ref[slot]


def gather_kernel(part0, part1, part2, part3, send_ref, wv_ref, dq_ref, att_ref, same_ref):
    summed = part0[...] + part1[...] + part2[...] + part3[...]
    wv_ref[...] = summed[0:64]
    dq_ref[...] = summed[64:80]
    for quarter in range(4):
        lanes = slice(128 * quarter, 128 * quarter + 128)
        att_ref[16 * quarter : 16 * quarter + 16] = summed[80:96, lanes]


def join_keys_kernel(keep_ref, recv_ref, mine_ref, other_ref, *parts):
    even = lax.rem(lax.axis_index("seq"), 2) == 0
    mine, other = mine_ref[...], other_ref[...]
    for slot, part in enumerate(parts):
        part[0:64] = keep_ref[slot] + recv_ref[slot]
        part[64:80] = jnp.where(even, mine, other)
        part[80:96] = jnp.where(even, other, mine)


def hist_grads(req, dk_ref, dv_ref, wk_ref, wv_ref, out_hbm, done_ref, buf, sems):
    copies = []
    for start in range(0, buf.shape[0], 512):
        rows = slice(start, start + 512)
        buf[rows] = (dot_last(dk_ref[req, rows], wk_ref[...])
                     + dot_last(dv_ref[req, rows], wv_ref[...])).astype(BF16)
        copy = pltpu.make_async_copy(buf.at[rows], out_hbm.at[req, rows], sems.at[len(copies)])
        copy.start()
        copies.append(copy)
    done_ref[...] = jnp.zeros(done_ref.shape, F32)
    for copy in copies:
        copy.wait()


def hist_grads_first_kernel(dk_ref, dv_ref, wk_ref, wv_ref, token_ref, *refs):
    hist_grads(0, dk_ref, dv_ref, wk_ref, wv_ref, *refs)


def hist_grads_second_kernel(dk_ref, dv_ref, wk_ref, wv_ref, token_ref, in_hbm, *refs):
    hist_grads(1, dk_ref, dv_ref, wk_ref, wv_ref, *refs)


def outer_kernel(*refs):
    keys = refs[0:4]
    wv_ref, tok_ref, att_ref, dout_ref, token_ref = refs[4:9]
    outs, (low_ref, dq_ref, all_ref) = refs[9:13], refs[13:]
    me = lax.axis_index("seq")
    for chips, part in enumerate(keys):
        dq_ref[lax.rem(me // 2 + 4 - chips, 4)] = part[64:96]
    dq = (dq_ref[...].reshape(128, 512) * 0.125).astype(BF16)
    low_ref[...] = dq
    row = lax.broadcasted_iota(jnp.int32, (64, 512), 0)
    col = lax.broadcasted_iota(jnp.int32, (64, 512), 1)
    feature = (row // 4) * 32 + me * 4 + row % 4
    pick = jnp.where(col == feature, 1.0, 0.0).astype(BF16)
    tok = dot_last(pick, tok_ref[...]).astype(BF16)
    parts = [dot(tok, dq),
             keys[0][0:64] + keys[1][0:64] + keys[2][0:64] + keys[3][0:64],
             wv_ref[...],
             dot(att_ref[...].astype(BF16), dout_ref[...])]
    for dp in range(16):
        for part in range(4):
            all_ref[dp, 4 * part : 4 * part + 4] = parts[part][4 * dp : 4 * dp + 4]
    y = lax.axis_index("dp") // 4
    for chips, out in enumerate(outs):
        out[...] = all_ref[pl.ds(4 * lax.rem(y + chips, 4), 4)]


def join_y_kernel(*refs):
    parts, outs, (sum_ref,) = refs[0:4], refs[5:9], refs[9:]
    sum_ref[...] = parts[0][...] + parts[1][...] + parts[2][...] + parts[3][...]
    x = lax.rem(lax.axis_index("dp"), 4)
    for chips, out in enumerate(outs):
        out[...] = sum_ref[lax.rem(x + chips, 4)]


def query_grad_kernel(dq_ref, wq_ref, out_ref):
    out_ref[...] = dot_last(dq_ref[...], wq_ref[...]).astype(BF16)


def final_kernel(part0, part1, part2, part3, out_hbm, out_ref, sem):
    summed = part0[...] + part1[...] + part2[...] + part3[...]
    for part in range(4):
        out_ref[:, part, :] = summed[4 * part : 4 * part + 4]
    copy = pltpu.make_async_copy(out_ref, out_hbm, sem)
    copy.start()
    copy.wait()


IN_VMEM = pl.BlockSpec(memory_space=VMEM)
IN_HBM = pl.BlockSpec(memory_space=pl.ANY)


def call(kernel, args, outs, scratch=(), aliases=(), limit=LIMIT):
    specs = {"vmem": IN_VMEM, "hbm": IN_HBM}
    spaces = {"vmem": VMEM, "hbm": HBM}
    ins = [pltpu.with_memory_space_constraint(x, spaces[s]) for x, s in args]
    return pl.pallas_call(
        kernel,
        in_specs=[specs[s] for _, s in args],
        out_specs=[specs[s] for s, _, _ in outs],
        out_shape=[spaces[s](shape, dtype) for s, dtype, shape in outs],
        scratch_shapes=scratch,
        input_output_aliases=dict(aliases),
        compiler_params=pltpu.CompilerParams(vmem_limit_bytes=limit * 1024 * 1024),
    )(*ins)


def turn(x, to):
    return lax.ppermute(x, "dp", [(i, to(i // 4, i % 4)) for i in range(16)])


def up(x, chips):
    return lax.ppermute(x, "seq", [(i, (i + 2 * chips) % 8) for i in range(8)])


def across(x):
    return lax.ppermute(x, "seq", [(i, i ^ 1) for i in range(8)])


def from_chips(x):
    return [x] + [up(x, chips) for chips in (1, 2, 3)]


def per_device(query_tokens, owner, d_out, history, lengths, w_query, w_key, w_value, w_out):
    rows, width = query_tokens.shape
    requests, events, _ = history.shape
    steps = events // TILE
    ev = (requests, events, width)
    mat = (width, width)
    blk = (PAIRS, 256, 256)
    vec = ("vmem", F32, (8, 256))
    pairs = (events, 256 * PAIRS)
    half = ("vmem", F32, (4, 64, width))
    quarter = ("vmem", F32, (64, width))
    wide_half = ("vmem", F32, (4, 96, width))
    wide = ("vmem", F32, (96, width))
    dma = pltpu.SemaphoreType.DMA
    v = lambda *xs: [(x, "vmem") for x in xs]
    h = lambda *xs: [(x, "hbm") for x in xs]

    keys, hist, stats, expo, tops, own, qbt = call(
        keys_kernel,
        h(lengths, owner.reshape(1, rows), query_tokens, w_query, w_key, history),
        [("vmem", BF16, ev), ("vmem", BF16, ev), vec, ("vmem", F32, pairs),
         ("vmem", F32, (steps, PAIRS, 256)), ("vmem", jnp.int32, (1, rows)), ("vmem", BF16, blk)],
        [pltpu.SMEM((requests,), jnp.int32), pltpu.VMEM((8, 256), jnp.int32),
         pltpu.VMEM(blk, BF16), pltpu.VMEM((rows, width), BF16),
         pltpu.VMEM(mat, BF16), pltpu.VMEM(mat, BF16), dma((5 + 2 * steps,))],
    )
    stats = from_chips(stats)
    (values,) = call(values_kernel, v(w_value, hist), [("vmem", BF16, ev)])
    (stats,) = call(join_stats_kernel, v(*stats, values), [vec])
    gb, gbt = call(
        out_grads_kernel, v(d_out, w_out, own, stats), [("vmem", BF16, blk), ("vmem", BF16, blk)])
    probs, slopes, delta = call(
        probs_kernel, v(stats, across(stats), expo, tops, gb, values),
        [("vmem", BF16, pairs), ("vmem", F32, pairs), vec])
    delta = from_chips(delta)
    dv, share = call(
        value_grads_kernel, v(probs, hist, gbt), [("vmem", BF16, ev), ("vmem", F32, (8, 64, width))],
        [pltpu.VMEM(mat, F32)])
    (delta,) = call(join_deltas_kernel, v(*delta, dv), [vec])
    (att,) = call(
        attention_kernel, v(own, probs, values, delta), [("vmem", F32, (8, 16, width))])

    ds, keep, send = call(
        query_part_kernel, v(delta, across(delta), own, probs, keys, slopes, att, share),
        [("vmem", BF16, pairs), wide_half, wide_half], [pltpu.VMEM((8, 16, width), F32)])
    (dk,) = call(key_grads_kernel, v(ds, qbt), [("vmem", BF16, ev)])
    parts = call(join_halves_kernel, v(keep, across(send), dk), [wide] * 4)
    token = parts[0]
    parts = [parts[0]] + [up(parts[i], i) for i in (1, 2, 3)]
    keep, send = call(
        key_weight_kernel, v(hist, dk, token), [half, half],
        [pltpu.VMEM(mat, F32), pltpu.VMEM((8, 64, width), F32)])
    wgrad_v, dq, att, send = call(
        gather_kernel, v(*parts, send),
        [quarter, ("vmem", F32, (16, width)), ("vmem", F32, (64, rows)), half], aliases={4: 3})
    parts = call(join_keys_kernel, v(keep, across(send), dq, across(dq)), [wide] * 4)
    token = parts[0]
    parts = [parts[0]] + [up(parts[i], i) for i in (1, 2, 3)]
    grad_out = [("hbm", BF16, ev), ("vmem", F32, (8, 128))]
    grad_scratch = [pltpu.VMEM((events, width), BF16), dma((events // 512,))]
    hist_grad, token = call(
        hist_grads_first_kernel, v(dk, dv, w_key, w_value, token), grad_out, grad_scratch)
    *outer, dq = call(
        outer_kernel, v(*parts, wgrad_v, query_tokens, att, d_out, token),
        [("vmem", F32, (4, 16, width))] * 4 + [("vmem", BF16, (rows, width))],
        [pltpu.VMEM((4, 32, width), F32), pltpu.VMEM((16, 16, width), F32)])
    outer = [outer[0]] + [turn(outer[i], lambda y, x: (y + i) % 4 * 4 + x) for i in (1, 2, 3)]
    hist_grad, token = call(
        hist_grads_second_kernel, v(dk, dv, w_key, w_value, dq) + h(hist_grad), grad_out,
        grad_scratch, aliases={5: 0})
    outer = call(
        join_y_kernel, v(*outer, token), [("vmem", F32, (16, width))] * 4,
        [pltpu.VMEM((4, 16, width), F32)])
    outer = [outer[0]] + [turn(outer[i], lambda y, x: y * 4 + (x + i) % 4) for i in (1, 2, 3)]
    (query_grad,) = call(
        query_grad_kernel, v(dq, w_query), [("vmem", BF16, (rows, width))])
    (weight_part,) = call(
        final_kernel, v(*outer), [("hbm", F32, (4, 4, width))],
        [pltpu.VMEM((4, 4, width), F32), dma])
    return query_grad, hist_grad, weight_part


def solution(mesh):
    return jax.shard_map(
        per_device,
        mesh=mesh,
        in_specs=(
            P("dp", None),
            P("dp"),
            P("dp", None),
            P("dp", "seq", None),
            P("dp"),
            P(),
            P(),
            P(),
            P(),
        ),
        out_specs=(P("dp", None), P("dp", "seq", None), P(("dp", "seq"), None, None)),
        check_vma=False,
    )
```

```python
import jax
import jax.numpy as jnp
from jax import lax
from jax.experimental import pallas as pl
from jax.experimental.pallas import tpu as pltpu
from jax.sharding import PartitionSpec as P

PAIRS = 4
LOW = -1e30
F32 = jnp.float32
BF16 = jnp.bfloat16
VMEM = pltpu.MemorySpace.VMEM
HBM = pltpu.MemorySpace.HBM
TILE = 1024
LIMIT = 8


def dot(left, right):
    return jnp.dot(left, right, preferred_element_type=F32)


def dot_last(left, right):
    return lax.dot_general(left, right, (((1,), (1,)), ((), ())), preferred_element_type=F32)


def dot_first(left, right):
    return lax.dot_general(left, right, (((0,), (0,)), ((), ())), preferred_element_type=F32)


def tiles(ref):
    events = ref.shape[1]
    return [slice(start, start + TILE) for start in range(0, events, TILE)]


def pair_cols(ref, pair, rows):
    cols = slice(128 * pair, 128 * pair + 128)
    return jnp.concatenate([ref[0, rows, cols], ref[1, rows, cols]], axis=1)


def put_pair(ref, pair, rows, value):
    cols = slice(128 * pair, 128 * pair + 128)
    ref[0, rows, cols] = value[:, 0:128]
    ref[1, rows, cols] = value[:, 128:256]


def pair_lanes(pair):
    return slice(256 * pair, 256 * pair + 256)


def seen_in(lim_ref, rows):
    place = lax.broadcasted_iota(jnp.int32, (rows.stop - rows.start, 256), 0) + rows.start
    return place < lim_ref[0:1]


def spread(full, own_col, owner_row, blk_ref, blk_t_ref):
    lane = lax.broadcasted_iota(jnp.int32, (128, 128), 1)
    zero = jnp.zeros((64, 128), F32)
    for pair in range(PAIRS):
        part = full[:, 128 * pair : 128 * pair + 128]
        part_t = part.T
        for req in range(2):
            mine = jnp.where(own_col == req, part, 0.0)
            cols = slice(128 * req, 128 * req + 128)
            blk_t_ref[pair, 0:128, cols] = jnp.where(lane < 64, mine, 0.0).astype(BF16)
            blk_t_ref[pair, 128:256, cols] = jnp.where(lane < 64, 0.0, mine).astype(BF16)
            mine_t = jnp.where(owner_row == req, part_t, 0.0)
            top = jnp.concatenate([mine_t[0:64], zero], axis=1)
            low = jnp.concatenate([zero, mine_t[64:128]], axis=1)
            blk_ref[pair, cols, :] = jnp.concatenate([top, low], axis=0).astype(BF16)


def keys_kernel(lens_hbm, own_hbm, tok_hbm, wq_hbm, wk_hbm, hist_hbm,
                key_ref, hist_ref, stat_ref, expo_ref, top_ref, own_ref, qbt_ref,
                lens_ref, lim_ref, qb_ref, tok_ref, wq_ref, wk_ref, sems):
    small = [(wq_hbm, wq_ref), (tok_hbm, tok_ref), (own_hbm, own_ref), (lens_hbm, lens_ref),
             (wk_hbm, wk_ref)]
    small = [pltpu.make_async_copy(src, dst, sems.at[i]) for i, (src, dst) in enumerate(small)]
    for copy in small:
        copy.start()
    chunks = []
    blocks = [slice(0, 512), slice(512, 1536), slice(1536, 2048)]
    for rows in blocks:
        for req in range(2):
            copy = pltpu.make_async_copy(
                hist_hbm.at[req, rows], hist_ref.at[req, rows], sems.at[5 + len(chunks)])
            copy.start()
            chunks.append(copy)
    for copy in small[0:4]:
        copy.wait()
    owner_row = jnp.broadcast_to(own_ref[...], (128, 128))
    base = lax.axis_index("seq") * hist_ref.shape[1]
    lim = jnp.where(own_ref[...] == 0, lens_ref[0], lens_ref[1]) - base
    lim_ref[...] = jnp.broadcast_to(jnp.concatenate([lim, lim], axis=1), (8, 256))
    q = dot(tok_ref[...], wq_ref[...]).astype(BF16).astype(F32) * 0.125
    spread(q, owner_row.T, owner_row[0:1], qb_ref, qbt_ref)
    small[4].wait()
    tops = [[] for _ in range(PAIRS)]
    sums = [[] for _ in range(PAIRS)]

    def project(rows):
        for req in range(2):
            key_ref[req, rows] = dot(hist_ref[req, rows], wk_ref[...]).astype(BF16)

    def score_tile(rows, pair):
        seen = seen_in(lim_ref, rows)
        score = jnp.where(seen, dot(pair_cols(key_ref, pair, rows), qb_ref[pair]), LOW)
        top = jnp.max(score, axis=0, keepdims=True)
        expo = jnp.exp(score - top)
        expo_ref[rows, pair_lanes(pair)] = expo
        tops[pair].append(top)
        sums[pair].append(jnp.sum(expo, axis=0, keepdims=True))

    waiting = []
    for index, rows in enumerate(blocks):
        chunks[2 * index].wait()
        chunks[2 * index + 1].wait()
        size = 256 if len(waiting) == PAIRS else 128
        starts = list(range(rows.start, rows.stop, size)) if waiting else []
        if not waiting:
            project(rows)
        every = max(len(waiting) // max(len(starts), 1), 1)
        for count, item in enumerate(waiting):
            if count % every == 0:
                start = starts[count // every]
                project(slice(start, start + size))
            score_tile(*item)
        waiting = [(slice(start, start + TILE // 2), pair)
                   for start in range(rows.start, rows.stop, TILE // 2) for pair in range(PAIRS)]
    for item in waiting:
        score_tile(*item)
    peaks, totals = [], []
    for pair in range(PAIRS):
        peak = tops[pair][0]
        for top in tops[pair][1:]:
            peak = jnp.maximum(peak, top)
        peaks.append(peak)
        totals.append(sum(x * jnp.exp(top - peak) for x, top in zip(sums[pair], tops[pair])))
    stat_ref[...] = jnp.concatenate(peaks + totals, axis=0)
    for pair in range(PAIRS):
        for index, top in enumerate(tops[pair]):
            top_ref[index, pair : pair + 1] = top


def values_kernel(wv_ref, hist_ref, val_ref):
    for rows in tiles(hist_ref):
        for req in range(2):
            val_ref[req, rows] = dot(hist_ref[req, rows], wv_ref[...]).astype(BF16)


def join_stats_kernel(*refs):
    stats, out_ref = refs[0:4], refs[-1]
    top = stats[0][0:4]
    for stat in stats[1:]:
        top = jnp.maximum(top, stat[0:4])
    norm = jnp.zeros((4, 256), F32)
    for stat in stats:
        norm += stat[4:8] * jnp.exp(stat[0:4] - top)
    out_ref[...] = jnp.concatenate([top, norm], axis=0)


def join_deltas_kernel(*refs):
    refs[-1][...] = refs[0][...] + refs[1][...] + refs[2][...] + refs[3][...]


def out_grads_kernel(dout_ref, wout_ref, own_ref, token_ref, gb_ref, gbt_ref):
    owner_row = jnp.broadcast_to(own_ref[...], (128, 128))
    g = dot_last(dout_ref[...], wout_ref[...]).astype(BF16).astype(F32)
    spread(g, owner_row.T, owner_row[0:1], gb_ref, gbt_ref)


def probs_kernel(one_ref, two_ref, expo_ref, top_ref, gb_ref, val_ref, prob_ref, slope_ref, delta_ref):
    one, two = one_ref[0:4], two_ref[0:4]
    top = jnp.maximum(one, two)
    norm = one_ref[4:8] * jnp.exp(one - top) + two_ref[4:8] * jnp.exp(two - top)
    shift = top + jnp.log(norm)
    delta = [jnp.zeros((1, 256), F32) for _ in range(PAIRS)]
    for index in range(top_ref.shape[0]):
        rows = slice(index * (TILE // 2), (index + 1) * (TILE // 2))
        factor = jnp.exp(top_ref[index] - shift)
        for pair in range(PAIRS):
            lanes = pair_lanes(pair)
            prob = (expo_ref[rows, lanes] * factor[pair : pair + 1]).astype(BF16)
            prob_ref[rows, lanes] = prob
            slope = dot(pair_cols(val_ref, pair, rows), gb_ref[pair])
            slope_ref[rows, lanes] = slope
            delta[pair] += jnp.sum(prob.astype(F32) * slope, axis=0, keepdims=True)
    delta_ref[...] = jnp.concatenate(delta + [jnp.zeros((4, 256), F32)], axis=0)


def put_shares(out_ref, value):
    for row in range(0, 512, 4):
        dp, seq = row // 32, (row // 4) % 8
        out_ref[seq, 4 * dp : 4 * dp + 4] = value[row : row + 4]


def put_shares(out_ref, value):
    for row in range(0, 512, 4):
        dp, seq = row // 32, (row // 4) % 8
        out_ref[seq, 4 * dp : 4 * dp + 4] = value[row : row + 4]


def halve(shares, keep_ref, send_ref, rows):
    me = lax.axis_index("seq")
    for slot in range(4):
        chip = lax.rem(me // 2 + slot, 4)
        keep_ref[slot, rows] = shares[2 * chip + lax.rem(me, 2)]
        send_ref[slot, rows] = shares[2 * chip + 1 - lax.rem(me, 2)]


def value_grads_kernel(prob_ref, hist_ref, gbt_ref, dv_ref, share_ref, wgrad):
    for rows in tiles(hist_ref):
        for pair in range(PAIRS):
            grad = dot(prob_ref[rows, pair_lanes(pair)], gbt_ref[pair]).astype(BF16)
            put_pair(dv_ref, pair, rows, grad)
    wgrad[...] = dot_first(hist_ref[0], dv_ref[0])
    wgrad[...] += dot_first(hist_ref[1], dv_ref[1])
    put_shares(share_ref, wgrad)


def attention_kernel(own_ref, prob_ref, val_ref, token_ref, att_ref):
    first = own_ref[...] == 0
    for pair in range(PAIRS):
        blk = jnp.zeros((256, 256), F32)
        for rows in tiles(val_ref):
            blk += dot_first(pair_cols(val_ref, pair, rows), prob_ref[rows, pair_lanes(pair)])
        for head in range(2):
            lanes = slice(128 * head, 128 * head + 128)
            one = blk[64 * head : 64 * head + 64, lanes]
            two = blk[128 + 64 * head : 192 + 64 * head, lanes]
            out = jnp.where(first, one, two)
            for row in range(0, 64, 4):
                feature = 128 * pair + 64 * head + row
                dp, seq = feature // 32, (feature // 4) % 8
                start = 4 * (dp % 4)
                att_ref[seq, start : start + 4, 128 * (dp // 4) : 128 * (dp // 4) + 128] = (
                    out[row : row + 4])


def query_part_kernel(one_ref, two_ref, own_ref, prob_ref, key_ref, slope_ref, att_ref,
                      share_ref, ds_ref, keep_ref, send_ref, dq_ref):
    delta = one_ref[...] + two_ref[...]
    own_col = jnp.broadcast_to(own_ref[...], (128, 128)).T
    lane = lax.broadcasted_iota(jnp.int32, (128, 128), 1)
    blks = [jnp.zeros((256, 256), F32) for _ in range(PAIRS)]
    for rows in tiles(key_ref):
        for pair in range(PAIRS):
            prob = prob_ref[rows, pair_lanes(pair)].astype(F32)
            slope = slope_ref[rows, pair_lanes(pair)]
            ds = (prob * (slope - delta[pair : pair + 1])).astype(BF16)
            ds_ref[rows, pair_lanes(pair)] = ds
            blks[pair] += dot_first(ds, pair_cols(key_ref, pair, rows))
    for pair in range(PAIRS):
        blk = blks[pair]
        one = jnp.where(own_col == 0, blk[:128, :128], blk[:128, 128:])
        two = jnp.where(own_col == 0, blk[128:, :128], blk[128:, 128:])
        dq = jnp.where(lane < 64, one, two)
        for dev in range(8):
            dq_ref[dev, :, 128 * pair : 128 * pair + 128] = dq[16 * dev : 16 * dev + 16]
    halve(share_ref, keep_ref, send_ref, slice(0, 64))
    halve(dq_ref, keep_ref, send_ref, slice(64, 80))
    halve(att_ref, keep_ref, send_ref, slice(80, 96))


def key_grads_kernel(ds_ref, qbt_ref, dk_ref):
    for rows in tiles(dk_ref):
        for pair in range(PAIRS):
            grad = dot(ds_ref[rows, pair_lanes(pair)], qbt_ref[pair]).astype(BF16)
            put_pair(dk_ref, pair, rows, grad)


def key_weight_kernel(hist_ref, dk_ref, token_ref, keep_ref, send_ref, wgrad, shares):
    wgrad[...] = dot_first(hist_ref[0], dk_ref[0])
    wgrad[...] += dot_first(hist_ref[1], dk_ref[1])
    put_shares(shares, wgrad)
    halve(shares, keep_ref, send_ref, slice(0, 64))


def join_halves_kernel(keep_ref, recv_ref, token_ref, *parts):
    for slot, part in enumerate(parts):
        part[...] = keep_ref[slot] + recv_ref[slot]


def gather_kernel(part0, part1, part2, part3, send_ref, wv_ref, dq_ref, att_ref, same_ref):
    summed = part0[...] + part1[...] + part2[...] + part3[...]
    wv_ref[...] = summed[0:64]
    dq_ref[...] = summed[64:80]
    for quarter in range(4):
        lanes = slice(128 * quarter, 128 * quarter + 128)
        att_ref[16 * quarter : 16 * quarter + 16] = summed[80:96, lanes]


def join_keys_kernel(keep_ref, recv_ref, mine_ref, other_ref, *parts):
    even = lax.rem(lax.axis_index("seq"), 2) == 0
    mine, other = mine_ref[...], other_ref[...]
    for slot, part in enumerate(parts):
        part[0:64] = keep_ref[slot] + recv_ref[slot]
        part[64:80] = jnp.where(even, mine, other)
        part[80:96] = jnp.where(even, other, mine)


def hist_grads(req, dk_ref, dv_ref, wk_ref, wv_ref, out_hbm, done_ref, buf, sems):
    copies = []
    for start in range(0, buf.shape[0], 512):
        rows = slice(start, start + 512)
        buf[rows] = (dot_last(dk_ref[req, rows], wk_ref[...])
                     + dot_last(dv_ref[req, rows], wv_ref[...])).astype(BF16)
        copy = pltpu.make_async_copy(buf.at[rows], out_hbm.at[req, rows], sems.at[len(copies)])
        copy.start()
        copies.append(copy)
    done_ref[...] = jnp.zeros(done_ref.shape, F32)
    for copy in copies:
        copy.wait()


def hist_grads_first_kernel(dk_ref, dv_ref, wk_ref, wv_ref, token_ref, *refs):
    hist_grads(0, dk_ref, dv_ref, wk_ref, wv_ref, *refs)


def hist_grads_second_kernel(dk_ref, dv_ref, wk_ref, wv_ref, token_ref, in_hbm, *refs):
    hist_grads(1, dk_ref, dv_ref, wk_ref, wv_ref, *refs)


def outer_kernel(*refs):
    keys = refs[0:4]
    wv_ref, tok_ref, att_ref, dout_ref, token_ref = refs[4:9]
    outs, (low_ref, dq_ref, all_ref) = refs[9:13], refs[13:]
    me = lax.axis_index("seq")
    for chips, part in enumerate(keys):
        dq_ref[lax.rem(me // 2 + 4 - chips, 4)] = part[64:96]
    dq = (dq_ref[...].reshape(128, 512) * 0.125).astype(BF16)
    low_ref[...] = dq
    row = lax.broadcasted_iota(jnp.int32, (64, 512), 0)
    col = lax.broadcasted_iota(jnp.int32, (64, 512), 1)
    feature = (row // 4) * 32 + me * 4 + row % 4
    pick = jnp.where(col == feature, 1.0, 0.0).astype(BF16)
    tok = dot_last(pick, tok_ref[...]).astype(BF16)
    parts = [dot(tok, dq),
             keys[0][0:64] + keys[1][0:64] + keys[2][0:64] + keys[3][0:64],
             wv_ref[...],
             dot(att_ref[...].astype(BF16), dout_ref[...])]
    for dp in range(16):
        for part in range(4):
            all_ref[dp, 4 * part : 4 * part + 4] = parts[part][4 * dp : 4 * dp + 4]
    y = lax.axis_index("dp") // 4
    for chips, out in enumerate(outs):
        out[...] = all_ref[pl.ds(4 * lax.rem(y + chips, 4), 4)]


def join_y_kernel(*refs):
    parts, outs, (sum_ref,) = refs[0:4], refs[5:9], refs[9:]
    sum_ref[...] = parts[0][...] + parts[1][...] + parts[2][...] + parts[3][...]
    x = lax.rem(lax.axis_index("dp"), 4)
    for chips, out in enumerate(outs):
        out[...] = sum_ref[lax.rem(x + chips, 4)]


def query_grad_kernel(dq_ref, wq_ref, out_ref):
    out_ref[...] = dot_last(dq_ref[...], wq_ref[...]).astype(BF16)


def final_kernel(part0, part1, part2, part3, out_hbm, out_ref, sem):
    summed = part0[...] + part1[...] + part2[...] + part3[...]
    for part in range(4):
        out_ref[:, part, :] = summed[4 * part : 4 * part + 4]
    copy = pltpu.make_async_copy(out_ref, out_hbm, sem)
    copy.start()
    copy.wait()


IN_VMEM = pl.BlockSpec(memory_space=VMEM)
IN_HBM = pl.BlockSpec(memory_space=pl.ANY)


def call(kernel, args, outs, scratch=(), aliases=(), limit=LIMIT):
    specs = {"vmem": IN_VMEM, "hbm": IN_HBM}
    spaces = {"vmem": VMEM, "hbm": HBM}
    ins = [pltpu.with_memory_space_constraint(x, spaces[s]) for x, s in args]
    return pl.pallas_call(
        kernel,
        in_specs=[specs[s] for _, s in args],
        out_specs=[specs[s] for s, _, _ in outs],
        out_shape=[spaces[s](shape, dtype) for s, dtype, shape in outs],
        scratch_shapes=scratch,
        input_output_aliases=dict(aliases),
        compiler_params=pltpu.CompilerParams(vmem_limit_bytes=limit * 1024 * 1024),
    )(*ins)


def turn(x, to):
    return lax.ppermute(x, "dp", [(i, to(i // 4, i % 4)) for i in range(16)])


def up(x, chips):
    return lax.ppermute(x, "seq", [(i, (i + 2 * chips) % 8) for i in range(8)])


def across(x):
    return lax.ppermute(x, "seq", [(i, i ^ 1) for i in range(8)])


def from_chips(x):
    return [x] + [up(x, chips) for chips in (1, 2, 3)]


def per_device(query_tokens, owner, d_out, history, lengths, w_query, w_key, w_value, w_out):
    rows, width = query_tokens.shape
    requests, events, _ = history.shape
    steps = events // TILE
    ev = (requests, events, width)
    mat = (width, width)
    blk = (PAIRS, 256, 256)
    vec = ("vmem", F32, (8, 256))
    pairs = (events, 256 * PAIRS)
    half = ("vmem", F32, (4, 64, width))
    quarter = ("vmem", F32, (64, width))
    wide_half = ("vmem", F32, (4, 96, width))
    wide = ("vmem", F32, (96, width))
    dma = pltpu.SemaphoreType.DMA
    v = lambda *xs: [(x, "vmem") for x in xs]
    h = lambda *xs: [(x, "hbm") for x in xs]

    keys, hist, stats, expo, tops, own, qbt = call(
        keys_kernel,
        h(lengths, owner.reshape(1, rows), query_tokens, w_query, w_key, history),
        [("vmem", BF16, ev), ("vmem", BF16, ev), vec, ("vmem", F32, pairs),
         ("vmem", F32, (2 * steps, PAIRS, 256)), ("vmem", jnp.int32, (1, rows)), ("vmem", BF16, blk)],
        [pltpu.SMEM((requests,), jnp.int32), pltpu.VMEM((8, 256), jnp.int32),
         pltpu.VMEM(blk, BF16), pltpu.VMEM((rows, width), BF16),
         pltpu.VMEM(mat, BF16), pltpu.VMEM(mat, BF16), dma((11,))],
    )
    stats = from_chips(stats)
    (values,) = call(values_kernel, v(w_value, hist), [("vmem", BF16, ev)])
    (stats,) = call(join_stats_kernel, v(*stats, values), [vec])
    gb, gbt = call(
        out_grads_kernel, v(d_out, w_out, own, stats), [("vmem", BF16, blk), ("vmem", BF16, blk)])
    probs, slopes, delta = call(
        probs_kernel, v(stats, across(stats), expo, tops, gb, values),
        [("vmem", BF16, pairs), ("vmem", F32, pairs), vec])
    delta = from_chips(delta)
    dv, share = call(
        value_grads_kernel, v(probs, hist, gbt), [("vmem", BF16, ev), ("vmem", F32, (8, 64, width))],
        [pltpu.VMEM(mat, F32)])
    (delta,) = call(join_deltas_kernel, v(*delta, dv), [vec])
    (att,) = call(
        attention_kernel, v(own, probs, values, delta), [("vmem", F32, (8, 16, width))])

    ds, keep, send = call(
        query_part_kernel, v(delta, across(delta), own, probs, keys, slopes, att, share),
        [("vmem", BF16, pairs), wide_half, wide_half], [pltpu.VMEM((8, 16, width), F32)])
    (dk,) = call(key_grads_kernel, v(ds, qbt), [("vmem", BF16, ev)])
    parts = call(join_halves_kernel, v(keep, across(send), dk), [wide] * 4)
    token = parts[0]
    parts = [parts[0]] + [up(parts[i], i) for i in (1, 2, 3)]
    keep, send = call(
        key_weight_kernel, v(hist, dk, token), [half, half],
        [pltpu.VMEM(mat, F32), pltpu.VMEM((8, 64, width), F32)])
    wgrad_v, dq, att, send = call(
        gather_kernel, v(*parts, send),
        [quarter, ("vmem", F32, (16, width)), ("vmem", F32, (64, rows)), half], aliases={4: 3})
    parts = call(join_keys_kernel, v(keep, across(send), dq, across(dq)), [wide] * 4)
    token = parts[0]
    parts = [parts[0]] + [up(parts[i], i) for i in (1, 2, 3)]
    grad_out = [("hbm", BF16, ev), ("vmem", F32, (8, 128))]
    grad_scratch = [pltpu.VMEM((events, width), BF16), dma((events // 512,))]
    hist_grad, token = call(
        hist_grads_first_kernel, v(dk, dv, w_key, w_value, token), grad_out, grad_scratch)
    *outer, dq = call(
        outer_kernel, v(*parts, wgrad_v, query_tokens, att, d_out, token),
        [("vmem", F32, (4, 16, width))] * 4 + [("vmem", BF16, (rows, width))],
        [pltpu.VMEM((4, 32, width), F32), pltpu.VMEM((16, 16, width), F32)])
    outer = [outer[0]] + [turn(outer[i], lambda y, x: (y + i) % 4 * 4 + x) for i in (1, 2, 3)]
    hist_grad, token = call(
        hist_grads_second_kernel, v(dk, dv, w_key, w_value, dq) + h(hist_grad), grad_out,
        grad_scratch, aliases={5: 0})
    outer = call(
        join_y_kernel, v(*outer, token), [("vmem", F32, (16, width))] * 4,
        [pltpu.VMEM((4, 16, width), F32)])
    outer = [outer[0]] + [turn(outer[i], lambda y, x: y * 4 + (x + i) % 4) for i in (1, 2, 3)]
    (query_grad,) = call(
        query_grad_kernel, v(dq, w_query), [("vmem", BF16, (rows, width))])
    (weight_part,) = call(
        final_kernel, v(*outer), [("hbm", F32, (4, 4, width))],
        [pltpu.VMEM((4, 4, width), F32), dma])
    return query_grad, hist_grad, weight_part


def solution(mesh):
    return jax.shard_map(
        per_device,
        mesh=mesh,
        in_specs=(
            P("dp", None),
            P("dp"),
            P("dp", None),
            P("dp", "seq", None),
            P("dp"),
            P(),
            P(),
            P(),
            P(),
        ),
        out_specs=(P("dp", None), P("dp", "seq", None), P(("dp", "seq"), None, None)),
        check_vma=False,
    )
```
